32 devices in a mesh: dp: 4 (over z), expert: 8 (over y, x, core).
Axes of the slice: x: 2, y: 2, z: 4, core: 2. Of those that a mesh axis runs over, the one named last changes fastest.
Arguments:
- tokens: bfloat16 [4096, 2560], P(('dp', 'expert')), may hold values from -6 to 6
- expert_ids: int32 [4096, 6], P(('dp', 'expert')), may hold values from 0 to 7, as said below
- gate_values: float32 [4096, 6], P(('dp', 'expert')), may hold values from 0.05 to 0.5
- w_gate: bfloat16 [8, 2560, 768], P('expert'), may hold values from -0.125 to 0.125
- w_up: bfloat16 [8, 2560, 768], P('expert'), may hold values from -0.125 to 0.125
- w_down: bfloat16 [8, 768, 2560], P('expert'), may hold values from -0.21875 to 0.21875
Outputs:
- moe_out: bfloat16 [4096, 2560], P(('dp', 'expert'))
The draws below stay inside these ranges and needn't reach their ends.
Inputs may be any that keep to these rules, and one draw needn't show every extreme that they name: `expert_ids`: within each block of 128 rows (one device's tokens), column 0 of every row holds one of two experts that are the same for all devices of a dp group, each of them in 56 to 72 rows, and no other entry names them; the two experts of different dp groups are different; the entries of a row differ; any other expert is named by at most 128 rows of one device, and in every dp group one such expert is named by exactly 128 rows of each of its devices; in some dp group other than the first, one of the two is named by 72 rows of every device, and that expert is named by exactly 128 rows of every device of the first dp group.
All inputs are finite; a program needn't handle non-finite values.
Results may differ from the reference program's by a relative error of at most 0.0058.
Values may be sent and summed in bfloat16 or wider, within the bound.
No kernel may reach another device: no remote copies, remote signals or barrier semaphores. Data moves between devices by JAX's collectives and lax.ppermute only.
A program may use at most 128 MiB of HBM per device.

```python
import jax
import jax.numpy as jnp
from jax import lax

D = 2560
F = 768
TOPK = 6
TOK_DEV = 128
EXPERTS = 8
ROWS = 4096
HOTMIN = 56
HOTMAX = 72
CAPN = 128
N_DP = 4
N_EXPERT = 8


def draw_expert_ids(key, part):
    others_count = EXPERTS - 2
    picks = 5 * TOK_DEV
    pool_size = others_count * CAPN
    global_order = jax.random.permutation(jax.random.fold_in(key, 5), EXPERTS).astype(jnp.int32)
    full_group = jax.random.randint(jax.random.fold_in(key, 7), (), 1, N_DP)
    target_side = jax.random.randint(jax.random.fold_in(key, 9), (), 0, 2)
    target = global_order[2 * full_group + target_side]

    def group_setup(group_number):
        group_key = jax.random.fold_in(key, 11 + group_number)
        base = jnp.arange(others_count, dtype=jnp.int32)
        mapped = base + 2 * (base >= 2 * group_number).astype(jnp.int32)
        shuffled = jax.random.permutation(group_key, others_count).astype(jnp.int32)
        others = global_order[mapped[shuffled]]
        favoured_pair = jnp.stack([global_order[2 * group_number], global_order[2 * group_number + 1]])
        ranking = jnp.concatenate([favoured_pair, others]).astype(jnp.int32)
        random_forced = jax.random.randint(jax.random.fold_in(group_key, 1), (), 0, others_count)
        target_place = jnp.argmax((others == target).astype(jnp.int32)).astype(jnp.int32)
        forced = jnp.where(group_number == 0, target_place, random_forced).astype(jnp.int32)
        return (ranking, forced)
    rankings, forced_all = jax.vmap(group_setup)(jnp.arange(N_DP, dtype=jnp.int32))

    def block_rows(block_number):
        group_number = block_number // N_EXPERT
        block_key = jax.random.fold_in(key, 1000 + block_number)
        ranking = rankings[group_number]
        forced = forced_all[group_number]
        favoured = jax.random.randint(jax.random.fold_in(block_key, 1), (), HOTMIN, HOTMAX + 1)
        favoured_first = jnp.where(group_number == full_group, jnp.where(target_side == 0, HOTMAX, HOTMIN), favoured)
        pool_ids = jnp.arange(pool_size, dtype=jnp.int32) // CAPN
        random_part = jax.random.randint(jax.random.fold_in(block_key, 2), (pool_size,), 1, 1024)
        scores = jnp.where(pool_ids == forced, 0, random_part) * pool_size + jnp.arange(pool_size, dtype=jnp.int32)
        chosen = jnp.sort(pool_ids[jnp.argsort(scores, stable=True)[:picks]])
        columns = chosen.reshape(5, TOK_DEV).T
        others = ranking[2 + columns]
        favoured_first = jnp.where((group_number == full_group) & (target_side == 1), TOK_DEV - HOTMAX, favoured_first)
        hot_column = jnp.where(jnp.arange(TOK_DEV) < favoured_first, ranking[0], ranking[1])
        rows_block = jnp.concatenate([hot_column[:, None], others], axis=1)
        token_order = jax.random.permutation(jax.random.fold_in(block_key, 3), TOK_DEV)
        return rows_block[token_order]
    every_block = jax.vmap(block_rows)(jnp.arange(N_DP * N_EXPERT, dtype=jnp.int32))
    return every_block.reshape(ROWS, TOPK).astype(jnp.int32)


def steps_of(own_key, shape, shards, smallest, largest):
    def one(axis_at, shards_of):
        steps = jax.random.uniform(jax.random.fold_in(jax.random.fold_in(own_key, 6), axis_at), (shards_of,), jnp.float32, smallest / len(shards), largest / len(shards))
        return jnp.repeat(jnp.exp(steps), shape[axis_at] // shards_of).reshape((-1,) + (1,) * (len(shape) - axis_at - 1))

    factor_of = one(*shards[0])
    for cut in shards[1:]:
        factor_of = factor_of * one(*cut)
    return factor_of


def centred(own_key, shape, spread, reach, pieces=(), held_as=jnp.bfloat16):
    level = steps_of(own_key, shape, pieces, -0.22, 0.18) if pieces else 1.0
    result = jax.random.normal(own_key, shape, jnp.float32) * spread * level
    return jnp.minimum(jnp.maximum(result, -reach), reach).astype(held_as)


def setup_inputs(seed: int = 0) -> dict:
    arg_keys = jax.random.split(jax.random.key(seed), 7)
    tokens = centred(arg_keys[0], (ROWS, D), 1.0, 6.0, ((0, 32),))
    expert_ids = draw_expert_ids(jax.random.fold_in(arg_keys[6], 71), 0)
    gate_values = jnp.clip(0.05 + 0.45 * jax.random.uniform(arg_keys[2], (ROWS, TOPK), jnp.float32) ** steps_of(arg_keys[2], (ROWS, TOPK), ((0, 32),), -0.2, 0.2), 0.05, 0.5)
    w_gate = centred(arg_keys[3], (EXPERTS, D, F), D ** -0.5, 0.125, ((0, 8),))
    w_up = centred(arg_keys[4], (EXPERTS, D, F), D ** -0.5, 0.125, ((0, 8),))
    w_down = centred(arg_keys[5], (EXPERTS, F, D), F ** -0.5, 0.21875, ((0, 8),))
    return {"tokens": tokens, "expert_ids": expert_ids, "gate_values": gate_values, "w_gate": w_gate, "w_up": w_up, "w_down": w_down}


def expert_apply(row_block, gate_matrix, up_matrix, down_matrix):
    gate_part = jnp.dot(row_block, gate_matrix, preferred_element_type=jnp.float32)
    up_part = jnp.dot(row_block, up_matrix, preferred_element_type=jnp.float32)
    hidden = (jax.nn.silu(gate_part) * up_part).astype(jnp.bfloat16)
    return jnp.dot(hidden, down_matrix, preferred_element_type=jnp.float32).astype(jnp.bfloat16)


def reference(tokens, expert_ids, gate_values, w_gate, w_up, w_down):
    flat_ids = expert_ids.reshape(-1).astype(jnp.int32)
    pair_count = flat_ids.shape[0]
    block_size = 256
    counts = jnp.zeros((EXPERTS,), jnp.int32).at[flat_ids].add(1)
    padded_counts = (counts + block_size - 1) // block_size * block_size
    starts = jnp.cumsum(counts) - counts
    padded_starts = jnp.cumsum(padded_counts) - padded_counts
    sorted_pairs = jnp.argsort(flat_ids, stable=True).astype(jnp.int32)
    flat_gates = gate_values.reshape(-1)
    block_total = (pair_count + block_size - 1) // block_size + EXPERTS

    def add_block(summed, block_number):
        block_start = block_number * block_size
        expert = (jnp.sum((padded_starts <= block_start).astype(jnp.int32)) - 1).astype(jnp.int32)
        within = block_start - padded_starts[expert] + jnp.arange(block_size, dtype=jnp.int32)
        in_range = within < counts[expert]
        pair_index = sorted_pairs[jnp.clip(starts[expert] + within, 0, pair_count - 1)]
        token_index = pair_index // TOPK
        outputs = expert_apply(tokens[token_index], w_gate[expert], w_up[expert], w_down[expert])
        weights = jnp.where(in_range, flat_gates[pair_index], jnp.zeros((), flat_gates.dtype))
        summed = summed.at[token_index].add(weights[:, None] * outputs.astype(summed.dtype))
        return summed, None

    summed, unused = lax.scan(add_block, jnp.zeros((ROWS, D), jnp.float32), jnp.arange(block_total, dtype=jnp.int32))
    return summed.astype(jnp.bfloat16)
```

```python
import functools

import jax
import jax.numpy as jnp
from jax import lax
from jax.experimental import pallas as pl
from jax.experimental.pallas import tpu as pltpu
from jax.sharding import PartitionSpec as P

CORE, X, Y = 1, 2, 4
LANES = 128
MIB = 2**20


def in_vmem(value):
    return pltpu.with_memory_space_constraint(value, pltpu.VMEM)


def whole():
    return pl.BlockSpec(memory_space=pltpu.VMEM)


def swap(value, offset):
    size = lax.axis_size("expert")
    return lax.ppermute(value, "expert", [(i, i ^ offset) for i in range(size)])


def pack_kernel(experts, tokens_ref, ids_ref, gates_ref, *out_refs):
    rows, features = tokens_ref.shape
    lane = lax.broadcasted_iota(jnp.int32, (rows, LANES), 1)
    expert = lane
    for _ in range(2):
        expert = jnp.where(expert >= experts, expert - experts, expert)
    weight = jnp.zeros((rows, LANES), jnp.float32)
    for k in range(ids_ref.shape[1]):
        weight += jnp.where(expert == ids_ref[:, k : k + 1], gates_ref[:, k : k + 1], 0.0)
    high = weight.astype(jnp.bfloat16).astype(jnp.float32)
    rest = weight - high
    middle = rest.astype(jnp.bfloat16).astype(jnp.float32)
    low = rest - middle
    terms = jnp.where(lane < experts, high, jnp.where(lane < 2 * experts, middle, low))
    terms = jnp.where(lane < 3 * experts, terms, 0.0).astype(jnp.bfloat16)
    start = 0
    for out_ref in out_refs:
        count = out_ref.shape[0]
        out_ref[:, :features] = tokens_ref[start : start + count, :]
        out_ref[:, features:] = terms[start : start + count, :]
        start += count


def pack(tokens, ids, gates, experts, parts):
    rows, features = tokens.shape
    shape = jax.ShapeDtypeStruct((rows // parts, features + LANES), tokens.dtype)
    return pl.pallas_call(
        functools.partial(pack_kernel, experts),
        out_shape=[shape] * parts,
        in_specs=[whole()] * 3,
        out_specs=[whole()] * parts,
        compiler_params=pltpu.CompilerParams(vmem_limit_bytes=16 * MIB),
        cost_estimate=pl.CostEstimate(flops=0, bytes_accessed=4 * rows * features, transcendentals=0),
        name="pack",
    )(tokens, ids, gates)


def expert_kernel(experts, count, has_before, *refs):
    index_ref, gate_ref, up_ref, down_ref = refs[:4]
    rows_refs = refs[4 : 4 + count]
    before_refs = refs[4 + count : 4 + 2 * count] if has_before else ()
    out_refs = refs[-1 - count : -1]
    hidden_ref = refs[-1]
    features, width = gate_ref.shape
    step = 256
    rows = jnp.concatenate([r[:, :features] for r in rows_refs], axis=0)
    terms = jnp.concatenate([r[:, features:] for r in rows_refs], axis=0).astype(jnp.float32)
    lane = lax.broadcasted_iota(jnp.int32, terms.shape, 1)
    own = index_ref[0]
    chosen = (lane == own) | (lane == own + experts) | (lane == own + 2 * experts)
    weight = jnp.sum(jnp.where(chosen, terms, 0.0), axis=1, keepdims=True)
    for at in range(0, width, step):
        gate = jnp.dot(rows, gate_ref[:, at : at + step], preferred_element_type=jnp.float32)
        up = jnp.dot(rows, up_ref[:, at : at + step], preferred_element_type=jnp.float32)
        hidden_ref[:, at : at + step] = (gate / (1.0 + jnp.exp(-gate)) * up).astype(jnp.bfloat16)
    hidden = hidden_ref[...]
    for at in range(0, features, 2 * step):
        columns = slice(at, at + 2 * step)
        answer = jnp.dot(hidden, down_ref[:, columns], preferred_element_type=jnp.float32) * weight
        start = 0
        for i, out_ref in enumerate(out_refs):
            stop = start + out_ref.shape[0]
            part = answer[start:stop]
            if has_before:
                part = part + before_refs[i][:, columns].astype(jnp.float32)
            out_ref[:, columns] = part.astype(out_ref.dtype)
            start = stop


def run_expert(weights, index, experts, rows, kinds, before=None):
    features, width = weights[0].shape
    total = sum(r.shape[0] for r in rows)
    operands = [in_vmem(w) for w in weights] + [in_vmem(r) for r in rows]
    if before is not None:
        operands += [in_vmem(b) for b in before]
    return pl.pallas_call(
        functools.partial(expert_kernel, experts, len(rows), before is not None),
        out_shape=[jax.ShapeDtypeStruct((r.shape[0], features), k) for r, k in zip(rows, kinds)],
        in_specs=[pl.BlockSpec(memory_space=pltpu.SMEM)] + [whole()] * len(operands),
        out_specs=[whole()] * len(rows),
        scratch_shapes=[pltpu.VMEM((total, width), jnp.bfloat16)],
        compiler_params=pltpu.CompilerParams(vmem_limit_bytes=16 * MIB),
        cost_estimate=pl.CostEstimate(
            flops=6 * total * features * width,
            bytes_accessed=total * features * 4,
            transcendentals=total * width,
        ),
        name="expert",
    )(index, *operands)


def sum_kernel(groups, *refs):
    out_ref = refs[-1]
    start = 0
    taken = 0
    for size, rows in groups:
        parts = [r[...].astype(jnp.float32) for r in refs[taken : taken + size]]
        total = parts[0]
        for part in parts[1:]:
            total = total + part
        out_ref[start : start + rows, :] = total.astype(out_ref.dtype)
        start += rows
        taken += size


def sums(groups):
    operands = [in_vmem(a) for group in groups for a in group]
    features = operands[0].shape[1]
    rows = sum(group[0].shape[0] for group in groups)
    return pl.pallas_call(
        functools.partial(sum_kernel, [(len(g), g[0].shape[0]) for g in groups]),
        out_shape=jax.ShapeDtypeStruct((rows, features), jnp.bfloat16),
        in_specs=[whole()] * len(operands),
        out_specs=whole(),
        compiler_params=pltpu.CompilerParams(vmem_limit_bytes=16 * MIB),
        cost_estimate=pl.CostEstimate(flops=rows * features, bytes_accessed=4 * rows * features, transcendentals=0),
        name="sums",
    )(*operands)


def on_four_chips(tokens, expert_ids, gate_values, w_gate, w_up, w_down):
    experts = lax.axis_size("expert")
    mine = lax.axis_index("expert").astype(jnp.int32).reshape(1)
    others = mine ^ CORE
    weights = (w_gate[0], w_up[0], w_down[0])
    own_a, own_b = pack(tokens, expert_ids, gate_values, experts, 2)
    x_a, y_a = swap(own_a, X), swap(own_a, Y)
    x_b, y_b = swap(own_b, X), swap(own_b, Y)
    far = tuple(swap(w, CORE) for w in weights)
    d_a, d_b = swap(x_a, Y), swap(y_b, X)

    wide, narrow = jnp.float32, jnp.bfloat16
    near_run = functools.partial(run_expert, weights, mine, experts)
    far_run = functools.partial(run_expert, far, others, experts)
    sum_own = near_run([own_a, own_b], [wide] * 2)
    first = near_run([x_a, y_a], [wide] * 2)
    second = near_run([x_b, y_b], [wide] * 2)
    sum_x_a, sum_y_a = far_run([x_a, y_a], [narrow, wide], first)
    sum_x_b, sum_y_b = far_run([x_b, y_b], [wide, narrow], second)
    back_x_a, back_y_b = swap(sum_x_a, X), swap(sum_y_b, Y)
    third = near_run([d_a, d_b], [wide] * 2)
    sum_d_a, sum_d_b = far_run([d_a, d_b], [narrow] * 2, third)
    via_x, via_y = swap(sum_d_a, X), swap(sum_d_b, Y)
    sum_own = far_run([own_a, own_b], [wide] * 2, sum_own)
    back_y_a = swap(sums([[sum_y_a, via_x]]), Y)
    back_x_b = swap(sums([[sum_x_b, via_y]]), X)
    return sums([[sum_own[0], back_x_a, back_y_a], [sum_own[1], back_x_b, back_y_b]])


def expert_apply(row_block, gate_matrix, up_matrix, down_matrix):
    gate_part = jnp.dot(row_block, gate_matrix, preferred_element_type=jnp.float32)
    up_part = jnp.dot(row_block, up_matrix, preferred_element_type=jnp.float32)
    hidden = (jax.nn.silu(gate_part) * up_part).astype(jnp.bfloat16)
    return jnp.dot(hidden, down_matrix, preferred_element_type=jnp.float32).astype(jnp.bfloat16)


def dispatched(tokens, expert_ids, gate_values, w_gate, w_up, w_down):
    token_count, features = tokens.shape
    topk_width = expert_ids.shape[1]
    experts_all = lax.axis_size("expert")
    pair_ids = expert_ids.reshape(-1)
    pair_rows = jnp.arange(pair_ids.shape[0], dtype=jnp.int32) // topk_width
    other_bound = min(
        token_count,
        ((topk_width - 1) * token_count + experts_all - 3) // (experts_all - 2) * 3 // 2,
    )
    slot_bound = max(token_count * 9 // 16, other_bound)
    one_hot = (pair_ids[:, None] == jnp.arange(experts_all, dtype=jnp.int32)[None, :]).astype(jnp.int32)
    earlier = jnp.cumsum(one_hot, axis=0) - one_hot
    places = pair_ids * slot_bound + jnp.sum(earlier * one_hot, axis=1)
    padded_source = jnp.concatenate([tokens, jnp.zeros((1, features), tokens.dtype)], axis=0)
    slot_table = (
        jnp.full((experts_all * slot_bound,), token_count, jnp.int32).at[places].set(pair_rows, mode="drop")
    )
    outgoing = padded_source[slot_table].reshape(experts_all, slot_bound, features)
    received = lax.all_to_all(outgoing, "expert", split_axis=0, concat_axis=0, tiled=True)
    answer = expert_apply(received.reshape(-1, features), w_gate[0], w_up[0], w_down[0])
    returned = lax.all_to_all(
        answer.reshape(received.shape), "expert", split_axis=0, concat_axis=0, tiled=True
    ).reshape(-1, features)[places]
    weighted = gate_values.reshape(-1)[:, None] * returned.astype(jnp.float32)
    return jnp.sum(weighted.reshape(token_count, topk_width, features), axis=1).astype(jnp.bfloat16)


def solution(mesh):
    placed = (
        P(("dp", "expert"), None),
        P(("dp", "expert"), None),
        P(("dp", "expert"), None),
        P("expert", None, None),
        P("expert", None, None),
        P("expert", None, None),
    )
    body = on_four_chips if mesh.shape["expert"] == 8 else dispatched
    return jax.shard_map(
        body, mesh=mesh, in_specs=placed, out_specs=P(("dp", "expert"), None), check_vma=False
    )
```

```python
import functools

import jax
import jax.numpy as jnp
from jax import lax
from jax.experimental import pallas as pl
from jax.experimental.pallas import tpu as pltpu
from jax.sharding import PartitionSpec as P

CORE, X, Y = 1, 2, 4
FIRST, SECOND = (X, Y), (Y, X)
LANES = 128
STEP = 256
MIB = 2**20


def in_vmem(value):
    return pltpu.with_memory_space_constraint(value, pltpu.VMEM)


def in_hbm(value):
    return pltpu.with_memory_space_constraint(value, pltpu.HBM)


def anywhere():
    return pl.BlockSpec(memory_space=pl.ANY)


def whole():
    return pl.BlockSpec(memory_space=pltpu.VMEM)


def swap(value, offsets):
    size = lax.axis_size("expert")
    return lax.ppermute(value, "expert", [(i, i ^ offsets[i % 2]) for i in range(size)])


def pack_kernel(experts, tokens_ref, ids_ref, gates_ref, out_ref, ids, gates, done):
    rows, features = tokens_ref.shape
    copies = [
        pltpu.make_async_copy(ids_ref, ids, done.at[0]),
        pltpu.make_async_copy(gates_ref, gates, done.at[1]),
        pltpu.make_async_copy(tokens_ref, out_ref.at[:, pl.ds(0, features)], done.at[2]),
    ]
    for copy in copies:
        copy.start()
    copies[0].wait()
    copies[1].wait()
    line = lax.broadcasted_iota(jnp.int32, (LANES, rows), 0)
    expert = line
    for _ in range(2):
        expert = jnp.where(expert >= experts, expert - experts, expert)
    weight = jnp.zeros((LANES, rows), jnp.float32)
    for k in range(ids_ref.shape[0]):
        weight += jnp.where(expert == ids[k : k + 1, :], gates[k : k + 1, :], 0.0)
    high = weight.astype(jnp.bfloat16).astype(jnp.float32)
    rest = weight - high
    middle = rest.astype(jnp.bfloat16).astype(jnp.float32)
    low = rest - middle
    terms = jnp.where(line < experts, high, jnp.where(line < 2 * experts, middle, low))
    terms = jnp.where(line < 3 * experts, terms, 0.0)
    out_ref[:, features:] = terms.T.astype(jnp.bfloat16)
    copies[2].wait()


def pack(tokens, ids, gates, experts):
    rows, features = tokens.shape
    ids, gates = ids.T, gates.T
    return pl.pallas_call(
        functools.partial(pack_kernel, experts),
        out_shape=jax.ShapeDtypeStruct((rows, features + LANES), tokens.dtype),
        in_specs=[anywhere()] * 3,
        out_specs=whole(),
        scratch_shapes=[
            pltpu.VMEM(ids.shape, ids.dtype),
            pltpu.VMEM(gates.shape, gates.dtype),
            pltpu.SemaphoreType.DMA((3,)),
        ],
        compiler_params=pltpu.CompilerParams(vmem_limit_bytes=8 * MIB),
        cost_estimate=pl.CostEstimate(flops=0, bytes_accessed=4 * rows * features, transcendentals=0),
        name="pack",
    )(in_hbm(tokens), in_hbm(ids), in_hbm(gates))


def row_weights(rows_ref, experts, features, other):
    terms = rows_ref[:, features:].astype(jnp.float32)
    lane = lax.broadcasted_iota(jnp.int32, terms.shape, 1)
    own = lax.axis_index("expert") ^ other
    chosen = (lane == own) | (lane == own + experts) | (lane == own + 2 * experts)
    return jnp.sum(jnp.where(chosen, terms, 0.0), axis=1, keepdims=True)


def hidden_columns(rows, gate_ref, up_ref, columns):
    gate = jnp.dot(rows, gate_ref[:, columns], preferred_element_type=jnp.float32)
    up = jnp.dot(rows, up_ref[:, columns], preferred_element_type=jnp.float32)
    return (gate / (1.0 + jnp.exp(-gate)) * up).astype(jnp.bfloat16)


def own_kernel(experts, gate_hbm, up_hbm, down_hbm, rows_ref, out_ref, gate_ref, up_ref, down_ref, hidden_ref, done):
    features, width = gate_ref.shape
    copies = []
    for at in range(0, width, STEP):
        columns = pl.ds(at, STEP)
        copies.append((gate_hbm.at[:, columns], gate_ref.at[:, columns]))
        copies.append((up_hbm.at[:, columns], up_ref.at[:, columns]))
    for at in range(0, features, 2 * STEP):
        columns = pl.ds(at, 2 * STEP)
        copies.append((down_hbm.at[:, columns], down_ref.at[:, columns]))
    copies = [pltpu.make_async_copy(a, b, done.at[i]) for i, (a, b) in enumerate(copies)]
    for copy in copies:
        copy.start()
    waits = iter(copies)
    rows = rows_ref[:, :features]
    weight = row_weights(rows_ref, experts, features, 0)
    for at in range(0, width, STEP):
        next(waits).wait()
        next(waits).wait()
        columns = slice(at, at + STEP)
        hidden_ref[:, columns] = hidden_columns(rows, gate_ref, up_ref, columns)
    hidden = hidden_ref[...]
    for at in range(0, features, 2 * STEP):
        next(waits).wait()
        columns = slice(at, at + 2 * STEP)
        out_ref[:, columns] = jnp.dot(hidden, down_ref[:, columns], preferred_element_type=jnp.float32) * weight


def run_own(weights, experts, rows):
    features, width = weights[0].shape
    count = rows.shape[0]
    copies = 2 * (width // STEP) + features // (2 * STEP)
    return pl.pallas_call(
        functools.partial(own_kernel, experts),
        out_shape=[jax.ShapeDtypeStruct((count, features), jnp.float32)]
        + [jax.ShapeDtypeStruct(w.shape, w.dtype) for w in weights],
        in_specs=[anywhere()] * 3 + [whole()],
        out_specs=[whole()] * 4,
        scratch_shapes=[pltpu.VMEM((count, width), jnp.bfloat16), pltpu.SemaphoreType.DMA((copies,))],
        compiler_params=pltpu.CompilerParams(vmem_limit_bytes=8 * MIB),
        cost_estimate=expert_cost(count, features, width),
        name="own",
    )(*[in_hbm(w) for w in weights], in_vmem(rows))


def expert_cost(count, features, width):
    return pl.CostEstimate(
        flops=6 * count * features * width, bytes_accessed=count * features * 4, transcendentals=count * width
    )


def expert_kernel(experts, other, added, *refs):
    gate_ref, up_ref, down_ref, rows_ref = refs[:4]
    out_ref, hidden_ref = refs[-2:]
    features, width = gate_ref.shape
    rows = rows_ref[:, :features]
    weight = row_weights(rows_ref, experts, features, other)
    for at in range(0, width, STEP):
        columns = slice(at, at + STEP)
        hidden_ref[:, columns] = hidden_columns(rows, gate_ref, up_ref, columns)
    hidden = hidden_ref[...]
    for at in range(0, features, 2 * STEP):
        columns = slice(at, at + 2 * STEP)
        answer = jnp.dot(hidden, down_ref[:, columns], preferred_element_type=jnp.float32) * weight
        for ref in refs[4 : 4 + added]:
            answer = answer + ref[:, columns].astype(jnp.float32)
        out_ref[:, columns] = answer.astype(out_ref.dtype)


def expert_and_rows_kernel(experts, other, added, *refs):
    expert_kernel(experts, other, added, *refs[:-2], refs[-1])


def run_expert(weights, other, experts, rows, kind, added=(), after=(), rows_too=False):
    features, width = weights[0].shape
    count = rows.shape[0]
    operands = [in_vmem(w) for w in (*weights, rows, *added)]
    specs = [whole()] * len(operands) + [anywhere()] * len(after)
    shapes = [jax.ShapeDtypeStruct((count, features), kind)]
    if rows_too:
        shapes.append(jax.ShapeDtypeStruct(rows.shape, rows.dtype))
    results = pl.pallas_call(
        functools.partial(expert_and_rows_kernel if rows_too else expert_kernel, experts, other, len(added)),
        out_shape=shapes,
        in_specs=specs,
        out_specs=[whole()] * len(shapes),
        input_output_aliases={3: 1} if rows_too else {},
        scratch_shapes=[pltpu.VMEM((count, width), jnp.bfloat16)],
        compiler_params=pltpu.CompilerParams(vmem_limit_bytes=8 * MIB),
        cost_estimate=expert_cost(count, features, width),
        name="expert",
    )(*operands, *after)
    return results if rows_too else results[0]


def sum_kernel(count, *refs):
    total = refs[0][...].astype(jnp.float32)
    for ref in refs[1:count]:
        total = total + ref[...].astype(jnp.float32)
    refs[-1][...] = total.astype(refs[-1].dtype)


def sums(*parts, after=()):
    rows, features = parts[0].shape
    return pl.pallas_call(
        functools.partial(sum_kernel, len(parts)),
        out_shape=jax.ShapeDtypeStruct((rows, features), jnp.bfloat16),
        in_specs=[whole()] * len(parts) + [anywhere()] * len(after),
        out_specs=whole(),
        compiler_params=pltpu.CompilerParams(vmem_limit_bytes=8 * MIB),
        cost_estimate=pl.CostEstimate(flops=rows * features, bytes_accessed=4 * rows * features, transcendentals=0),
        name="sums",
    )(*[in_vmem(p) for p in parts], *after)


def on_four_chips(tokens, expert_ids, gate_values, w_gate, w_up, w_down):
    experts = lax.axis_size("expert")
    weights = (w_gate[0], w_up[0], w_down[0])
    far = tuple(swap(w, (CORE, CORE)) for w in weights)
    own = pack(tokens, expert_ids, gate_values, experts)
    first = swap(own, FIRST)
    second = swap(own, SECOND)

    wide, narrow = jnp.float32, jnp.bfloat16
    near_own, *near = run_own(weights, experts, own)
    near_run = functools.partial(run_expert, near, 0, experts)
    far_run = functools.partial(run_expert, far, CORE, experts)
    near_first, first = near_run(first, wide, after=[near_own], rows_too=True)
    third = swap(first, SECOND)
    near_second = near_run(second, wide, after=[near_first])
    sum_second = far_run(second, narrow, [near_second])
    back_second = swap(sum_second, SECOND)
    near_third = near_run(third, wide, after=[sum_second])
    sum_third = far_run(third, narrow, [near_third])
    passed = swap(sum_third, SECOND)
    sum_first = far_run(first, wide, [near_first], after=[sum_third])
    sum_own = far_run(own, wide, [near_own, back_second], after=[sum_first])
    back_first = swap(sums(sum_first, passed, after=[sum_own]), FIRST)
    return sums(sum_own, back_first)


def expert_apply(row_block, gate_matrix, up_matrix, down_matrix):
    gate_part = jnp.dot(row_block, gate_matrix, preferred_element_type=jnp.float32)
    up_part = jnp.dot(row_block, up_matrix, preferred_element_type=jnp.float32)
    hidden = (jax.nn.silu(gate_part) * up_part).astype(jnp.bfloat16)
    return jnp.dot(hidden, down_matrix, preferred_element_type=jnp.float32).astype(jnp.bfloat16)


def dispatched(tokens, expert_ids, gate_values, w_gate, w_up, w_down):
    token_count, features = tokens.shape
    topk_width = expert_ids.shape[1]
    experts_all = lax.axis_size("expert")
    pair_ids = expert_ids.reshape(-1)
    pair_rows = jnp.arange(pair_ids.shape[0], dtype=jnp.int32) // topk_width
    other_bound = min(
        token_count,
        ((topk_width - 1) * token_count + experts_all - 3) // (experts_all - 2) * 3 // 2,
    )
    slot_bound = max(token_count * 9 // 16, other_bound)
    one_hot = (pair_ids[:, None] == jnp.arange(experts_all, dtype=jnp.int32)[None, :]).astype(jnp.int32)
    earlier = jnp.cumsum(one_hot, axis=0) - one_hot
    places = pair_ids * slot_bound + jnp.sum(earlier * one_hot, axis=1)
    padded_source = jnp.concatenate([tokens, jnp.zeros((1, features), tokens.dtype)], axis=0)
    slot_table = (
        jnp.full((experts_all * slot_bound,), token_count, jnp.int32).at[places].set(pair_rows, mode="drop")
    )
    outgoing = padded_source[slot_table].reshape(experts_all, slot_bound, features)
    received = lax.all_to_all(outgoing, "expert", split_axis=0, concat_axis=0, tiled=True)
    answer = expert_apply(received.reshape(-1, features), w_gate[0], w_up[0], w_down[0])
    returned = lax.all_to_all(
        answer.reshape(received.shape), "expert", split_axis=0, concat_axis=0, tiled=True
    ).reshape(-1, features)[places]
    weighted = gate_values.reshape(-1)[:, None] * returned.astype(jnp.float32)
    return jnp.sum(weighted.reshape(token_count, topk_width, features), axis=1).astype(jnp.bfloat16)


def solution(mesh):
    placed = (
        P(("dp", "expert"), None),
        P(("dp", "expert"), None),
        P(("dp", "expert"), None),
        P("expert", None, None),
        P("expert", None, None),
        P("expert", None, None),
    )
    body = on_four_chips if mesh.shape["expert"] == 8 else dispatched
    return jax.shard_map(
        body, mesh=mesh, in_specs=placed, out_specs=P(("dp", "expert"), None), check_vma=False
    )
```

```python
import functools

import jax
import jax.numpy as jnp
from jax import lax
from jax.experimental import pallas as pl
from jax.experimental.pallas import tpu as pltpu
from jax.sharding import PartitionSpec as P

CORE, X, Y = 1, 2, 4
FIRST, SECOND = (X, Y), (Y, X)
LANES = 128
STEP = 256
MIB = 2**20


def in_vmem(value):
    return pltpu.with_memory_space_constraint(value, pltpu.VMEM)


def in_hbm(value):
    return pltpu.with_memory_space_constraint(value, pltpu.HBM)


def anywhere():
    return pl.BlockSpec(memory_space=pl.ANY)


def whole():
    return pl.BlockSpec(memory_space=pltpu.VMEM)


def swap(value, offsets):
    size = lax.axis_size("expert")
    return lax.ppermute(value, "expert", [(i, i ^ offsets[i % 2]) for i in range(size)])


def pack_kernel(experts, tokens_ref, ids_ref, gates_ref, out_ref, again_ref, ids, gates, done):
    rows, features = tokens_ref.shape
    copies = [
        pltpu.make_async_copy(ids_ref, ids, done.at[0]),
        pltpu.make_async_copy(gates_ref, gates, done.at[1]),
        pltpu.make_async_copy(tokens_ref, out_ref.at[:, pl.ds(0, features)], done.at[2]),
        pltpu.make_async_copy(tokens_ref, again_ref.at[:, pl.ds(0, features)], done.at[3]),
    ]
    for copy in copies:
        copy.start()
    copies[0].wait()
    copies[1].wait()
    line = lax.broadcasted_iota(jnp.int32, (LANES, rows), 0)
    expert = line
    for _ in range(2):
        expert = jnp.where(expert >= experts, expert - experts, expert)
    weight = jnp.zeros((LANES, rows), jnp.float32)
    for k in range(ids_ref.shape[0]):
        weight += jnp.where(expert == ids[k : k + 1, :], gates[k : k + 1, :], 0.0)
    high = weight.astype(jnp.bfloat16).astype(jnp.float32)
    rest = weight - high
    middle = rest.astype(jnp.bfloat16).astype(jnp.float32)
    low = rest - middle
    terms = jnp.where(line < experts, high, jnp.where(line < 2 * experts, middle, low))
    terms = jnp.where(line < 3 * experts, terms, 0.0)
    terms = terms.T.astype(jnp.bfloat16)
    out_ref[:, features:] = terms
    again_ref[:, features:] = terms
    copies[2].wait()
    copies[3].wait()


def pack(tokens, ids, gates, experts):
    rows, features = tokens.shape
    ids, gates = ids.T, gates.T
    return pl.pallas_call(
        functools.partial(pack_kernel, experts),
        out_shape=[jax.ShapeDtypeStruct((rows, features + LANES), tokens.dtype)] * 2,
        in_specs=[anywhere()] * 3,
        out_specs=[whole()] * 2,
        scratch_shapes=[
            pltpu.VMEM(ids.shape, ids.dtype),
            pltpu.VMEM(gates.shape, gates.dtype),
            pltpu.SemaphoreType.DMA((4,)),
        ],
        compiler_params=pltpu.CompilerParams(vmem_limit_bytes=16 * MIB),
        cost_estimate=pl.CostEstimate(flops=0, bytes_accessed=4 * rows * features, transcendentals=0),
        name="pack",
    )(in_hbm(tokens), in_hbm(ids), in_hbm(gates))


def row_weights(terms, experts, other):
    terms = terms.astype(jnp.float32)
    lane = lax.broadcasted_iota(jnp.int32, terms.shape, 1)
    own = lax.axis_index("expert") ^ other
    chosen = (lane == own) | (lane == own + experts) | (lane == own + 2 * experts)
    return jnp.sum(jnp.where(chosen, terms, 0.0), axis=1, keepdims=True)


def hidden_columns(rows, gate_ref, up_ref, columns):
    gate = jnp.dot(rows, gate_ref[:, columns], preferred_element_type=jnp.float32)
    up = jnp.dot(rows, up_ref[:, columns], preferred_element_type=jnp.float32)
    return (gate / (1.0 + jnp.exp(-gate)) * up).astype(jnp.bfloat16)


def own_kernel(experts, gate_hbm, up_hbm, down_hbm, rows_ref, out_ref, gate_ref, up_ref, down_ref, hidden_ref, done):
    features, width = gate_ref.shape
    copies = []
    for at in range(0, width, STEP):
        columns = pl.ds(at, STEP)
        copies.append((gate_hbm.at[:, columns], gate_ref.at[:, columns]))
        copies.append((up_hbm.at[:, columns], up_ref.at[:, columns]))
    for at in range(0, features, 2 * STEP):
        columns = pl.ds(at, 2 * STEP)
        copies.append((down_hbm.at[:, columns], down_ref.at[:, columns]))
    copies = [pltpu.make_async_copy(a, b, done.at[i]) for i, (a, b) in enumerate(copies)]
    for copy in copies:
        copy.start()
    waits = iter(copies)
    rows = rows_ref[:, :features]
    weight = row_weights(rows_ref[:, features:], experts, 0)
    for at in range(0, width, STEP):
        next(waits).wait()
        next(waits).wait()
        columns = slice(at, at + STEP)
        hidden_ref[:, columns] = hidden_columns(rows, gate_ref, up_ref, columns)
    hidden = hidden_ref[...]
    for at in range(0, features, 2 * STEP):
        next(waits).wait()
        columns = slice(at, at + 2 * STEP)
        out_ref[:, columns] = jnp.dot(hidden, down_ref[:, columns], preferred_element_type=jnp.float32) * weight


def run_own(weights, experts, rows):
    features, width = weights[0].shape
    count = rows.shape[0]
    copies = 2 * (width // STEP) + features // (2 * STEP)
    return pl.pallas_call(
        functools.partial(own_kernel, experts),
        out_shape=[jax.ShapeDtypeStruct((count, features), jnp.float32)]
        + [jax.ShapeDtypeStruct(w.shape, w.dtype) for w in weights],
        in_specs=[anywhere()] * 3 + [whole()],
        out_specs=[whole()] * 4,
        scratch_shapes=[pltpu.VMEM((count, width), jnp.bfloat16), pltpu.SemaphoreType.DMA((copies,))],
        compiler_params=pltpu.CompilerParams(vmem_limit_bytes=16 * MIB),
        cost_estimate=expert_cost(count, features, width),
        name="own",
    )(*[in_hbm(w) for w in weights], in_vmem(rows))


def nothing(*refs):
    pass


def held(*values, after=()):
    return pl.pallas_call(
        nothing,
        out_shape=[jax.ShapeDtypeStruct(v.shape, v.dtype) for v in values],
        in_specs=[anywhere()] * (len(values) + len(after)),
        out_specs=[anywhere()] * len(values),
        input_output_aliases={i: i for i in range(len(values))},
        compiler_params=pltpu.CompilerParams(vmem_limit_bytes=MIB),
        cost_estimate=pl.CostEstimate(flops=0, bytes_accessed=0, transcendentals=0),
        name="held",
    )(*values, *after)


def expert_cost(count, features, width):
    return pl.CostEstimate(
        flops=6 * count * features * width, bytes_accessed=count * features * 4, transcendentals=count * width
    )


def expert_kernel(experts, other, added, after, parts, *refs):
    gate_ref, up_ref, down_ref, rows_ref = refs[:4]
    added_refs = refs[4 : 4 + added * parts]
    out_refs = refs[4 + added * parts + after : -1]
    hidden_ref = refs[-1]
    features, width = gate_ref.shape
    rows = rows_ref[:, :features]
    weight = row_weights(rows_ref[:, features:], experts, other)
    for at in range(0, width, STEP):
        columns = slice(at, at + STEP)
        hidden_ref[:, columns] = hidden_columns(rows, gate_ref, up_ref, columns)
    hidden = hidden_ref[...]
    for at in range(0, features, 2 * STEP):
        columns = slice(at, at + 2 * STEP)
        answer = jnp.dot(hidden, down_ref[:, columns], preferred_element_type=jnp.float32) * weight
        start = 0
        for i, out_ref in enumerate(out_refs):
            part = answer[start : start + out_ref.shape[0]]
            for ref in added_refs[i::parts]:
                part = part + ref[:, columns].astype(jnp.float32)
            out_ref[:, columns] = part.astype(out_ref.dtype)
            start += out_ref.shape[0]


def run_expert(weights, other, experts, rows, kind, *added, parts=1, after=()):
    features, width = weights[0].shape
    count = rows.shape[0]
    operands = [in_vmem(v) for v in (*weights, rows, *(v for group in added for v in group))]
    return pl.pallas_call(
        functools.partial(expert_kernel, experts, other, len(added), len(after), parts),
        out_shape=[jax.ShapeDtypeStruct((count // parts, features), kind)] * parts,
        in_specs=[whole()] * len(operands) + [anywhere()] * len(after),
        out_specs=[whole()] * parts,
        scratch_shapes=[pltpu.VMEM((count, width), jnp.bfloat16)],
        compiler_params=pltpu.CompilerParams(vmem_limit_bytes=16 * MIB),
        cost_estimate=expert_cost(count, features, width),
        name="expert",
    )(*operands, *after)


def sum_kernel(first_ref, second_ref, *refs):
    refs[-1][...] = (first_ref[...].astype(jnp.float32) + second_ref[...].astype(jnp.float32)).astype(refs[-1].dtype)


def sums(first, second, after=()):
    return pl.pallas_call(
        sum_kernel,
        out_shape=jax.ShapeDtypeStruct(first.shape, jnp.bfloat16),
        in_specs=[whole()] * 2 + [anywhere()] * len(after),
        out_specs=whole(),
        compiler_params=pltpu.CompilerParams(vmem_limit_bytes=16 * MIB),
        name="sums",
    )(in_vmem(first), in_vmem(second), *after)


def finish_kernel(whole_ref, upper_ref, lower_ref, out_ref):
    half = upper_ref.shape[0]
    out_ref[:half] = (whole_ref[:half] + upper_ref[...].astype(jnp.float32)).astype(out_ref.dtype)
    out_ref[half:] = (whole_ref[half:] + lower_ref[...].astype(jnp.float32)).astype(out_ref.dtype)


def finish(whole_part, upper, lower):
    return pl.pallas_call(
        finish_kernel,
        out_shape=jax.ShapeDtypeStruct(whole_part.shape, jnp.bfloat16),
        in_specs=[whole()] * 3,
        out_specs=whole(),
        compiler_params=pltpu.CompilerParams(vmem_limit_bytes=16 * MIB),
        name="finish",
    )(in_vmem(whole_part), in_vmem(upper), in_vmem(lower))


def on_four_chips(tokens, expert_ids, gate_values, w_gate, w_up, w_down):
    experts = lax.axis_size("expert")
    weights = (w_gate[0], w_up[0], w_down[0])
    far = tuple(swap(w, (CORE, CORE)) for w in weights)
    own, again = pack(tokens, expert_ids, gate_values, experts)
    wide, narrow = jnp.float32, jnp.bfloat16
    first = swap(own, FIRST)
    near_own, *near = run_own(weights, experts, own)
    second = swap(*held(again, after=[near_own]), SECOND)
    third = swap(first, SECOND)
    near_run = functools.partial(run_expert, near, 0, experts)
    far_run = functools.partial(run_expert, far, CORE, experts)
    near_second = near_run(second, wide, after=[near_own])
    sum_second = far_run(second, narrow, near_second)
    back_second = swap(sum_second[0], SECOND)
    near_third = near_run(third, wide, parts=2, after=sum_second)
    sum_third = far_run(third, narrow, near_third, parts=2)
    passed_a, passed_b = swap(sum_third[0], SECOND), swap(sum_third[1], SECOND)
    near_first = near_run(first, wide, parts=2, after=sum_third)
    sum_first = far_run(first, wide, near_first, parts=2)
    sum_own = far_run(own, wide, [near_own], [back_second], after=sum_first)[0]
    back_first_a = swap(sums(sum_first[0], passed_a, after=[sum_own]), FIRST)
    back_first_b = swap(sums(sum_first[1], passed_b, after=[sum_own]), FIRST)
    return finish(sum_own, back_first_a, back_first_b)


def expert_apply(row_block, gate_matrix, up_matrix, down_matrix):
    gate_part = jnp.dot(row_block, gate_matrix, preferred_element_type=jnp.float32)
    up_part = jnp.dot(row_block, up_matrix, preferred_element_type=jnp.float32)
    hidden = (jax.nn.silu(gate_part) * up_part).astype(jnp.bfloat16)
    return jnp.dot(hidden, down_matrix, preferred_element_type=jnp.float32).astype(jnp.bfloat16)


def dispatched(tokens, expert_ids, gate_values, w_gate, w_up, w_down):
    token_count, features = tokens.shape
    topk_width = expert_ids.shape[1]
    experts_all = lax.axis_size("expert")
    pair_ids = expert_ids.reshape(-1)
    pair_rows = jnp.arange(pair_ids.shape[0], dtype=jnp.int32) // topk_width
    other_bound = min(
        token_count,
        ((topk_width - 1) * token_count + experts_all - 3) // (experts_all - 2) * 3 // 2,
    )
    slot_bound = max(token_count * 9 // 16, other_bound)
    one_hot = (pair_ids[:, None] == jnp.arange(experts_all, dtype=jnp.int32)[None, :]).astype(jnp.int32)
    earlier = jnp.cumsum(one_hot, axis=0) - one_hot
    places = pair_ids * slot_bound + jnp.sum(earlier * one_hot, axis=1)
    padded_source = jnp.concatenate([tokens, jnp.zeros((1, features), tokens.dtype)], axis=0)
    slot_table = (
        jnp.full((experts_all * slot_bound,), token_count, jnp.int32).at[places].set(pair_rows, mode="drop")
    )
    outgoing = padded_source[slot_table].reshape(experts_all, slot_bound, features)
    received = lax.all_to_all(outgoing, "expert", split_axis=0, concat_axis=0, tiled=True)
    answer = expert_apply(received.reshape(-1, features), w_gate[0], w_up[0], w_down[0])
    returned = lax.all_to_all(
        answer.reshape(received.shape), "expert", split_axis=0, concat_axis=0, tiled=True
    ).reshape(-1, features)[places]
    weighted = gate_values.reshape(-1)[:, None] * returned.astype(jnp.float32)
    return jnp.sum(weighted.reshape(token_count, topk_width, features), axis=1).astype(jnp.bfloat16)


def solution(mesh):
    placed = (
        P(("dp", "expert"), None),
        P(("dp", "expert"), None),
        P(("dp", "expert"), None),
        P("expert", None, None),
        P("expert", None, None),
        P("expert", None, None),
    )
    body = on_four_chips if mesh.shape["expert"] == 8 else dispatched
    return jax.shard_map(
        body, mesh=mesh, in_specs=placed, out_specs=P(("dp", "expert"), None), check_vma=False
    )
```

```python
import functools

import jax
import jax.numpy as jnp
from jax import lax
from jax.experimental import pallas as pl
from jax.experimental.pallas import tpu as pltpu
from jax.sharding import PartitionSpec as P

CORE, X, Y = 1, 2, 4
FIRST, SECOND = (X, Y), (Y, X)
LANES = 128
STEP = 256
MIB = 2**20


def in_vmem(value):
    return pltpu.with_memory_space_constraint(value, pltpu.VMEM)


def in_hbm(value):
    return pltpu.with_memory_space_constraint(value, pltpu.HBM)


def anywhere():
    return pl.BlockSpec(memory_space=pl.ANY)


def whole():
    return pl.BlockSpec(memory_space=pltpu.VMEM)


def swap(value, offsets):
    size = lax.axis_size("expert")
    return lax.ppermute(value, "expert", [(i, i ^ offsets[i % 2]) for i in range(size)])


def row_terms(ids, gates, experts):
    topk, rows = ids.shape
    line = lax.broadcasted_iota(jnp.int32, (LANES, rows), 0)
    expert = line
    for _ in range(2):
        expert = jnp.where(expert >= experts, expert - experts, expert)
    weight = jnp.zeros((LANES, rows), jnp.float32)
    for k in range(topk):
        weight += jnp.where(expert == ids[k : k + 1, :], gates[k : k + 1, :], 0.0)
    high = weight.astype(jnp.bfloat16).astype(jnp.float32)
    rest = weight - high
    middle = rest.astype(jnp.bfloat16).astype(jnp.float32)
    low = rest - middle
    terms = jnp.where(line < experts, high, jnp.where(line < 2 * experts, middle, low))
    return jnp.where(line < 3 * experts, terms, 0.0).T.astype(jnp.bfloat16)


def row_weights(terms, experts, other):
    terms = terms.astype(jnp.float32)
    lane = lax.broadcasted_iota(jnp.int32, terms.shape, 1)
    own = lax.axis_index("expert") ^ other
    chosen = (lane == own) | (lane == own + experts) | (lane == own + 2 * experts)
    return jnp.sum(jnp.where(chosen, terms, 0.0), axis=1, keepdims=True)


def hidden_columns(rows, gate_ref, up_ref, columns):
    gate = jnp.dot(rows, gate_ref[:, columns], preferred_element_type=jnp.float32)
    up = jnp.dot(rows, up_ref[:, columns], preferred_element_type=jnp.float32)
    return (gate / (1.0 + jnp.exp(-gate)) * up).astype(jnp.bfloat16)


def own_hidden_kernel(
    experts, tokens_hbm, ids_hbm, gates_hbm, gate_hbm, up_hbm, rows_ref, terms_ref, hidden_ref, gate_ref, up_ref, ids, gates, done
):
    rows, features = tokens_hbm.shape
    width = gate_ref.shape[1]
    pairs = [(ids_hbm, ids), (gates_hbm, gates), (tokens_hbm, rows_ref.at[:, pl.ds(0, features)])]
    for at in range(0, width, STEP):
        columns = pl.ds(at, STEP)
        pairs.append((gate_hbm.at[:, columns], gate_ref.at[:, columns]))
        pairs.append((up_hbm.at[:, columns], up_ref.at[:, columns]))
    copies = [pltpu.make_async_copy(a, b, done.at[i]) for i, (a, b) in enumerate(pairs)]
    for copy in copies:
        copy.start()
    copies[0].wait()
    copies[1].wait()
    terms = row_terms(ids, gates, experts)
    terms_ref[...] = terms
    rows_ref[:, features:] = terms
    copies[2].wait()
    rows = rows_ref[:, :features]
    waits = iter(copies[3:])
    for at in range(0, width, STEP):
        next(waits).wait()
        next(waits).wait()
        columns = slice(at, at + STEP)
        hidden_ref[:, columns] = hidden_columns(rows, gate_ref, up_ref, columns)


def own_hidden(tokens, ids, gates, gate, up, experts):
    count, features = tokens.shape
    width = gate.shape[1]
    ids, gates = ids.T, gates.T
    return pl.pallas_call(
        functools.partial(own_hidden_kernel, experts),
        out_shape=[
            jax.ShapeDtypeStruct((count, features + LANES), tokens.dtype),
            jax.ShapeDtypeStruct((count, LANES), tokens.dtype),
            jax.ShapeDtypeStruct((count, width), tokens.dtype),
            jax.ShapeDtypeStruct(gate.shape, gate.dtype),
            jax.ShapeDtypeStruct(up.shape, up.dtype),
        ],
        in_specs=[anywhere()] * 5,
        out_specs=[whole()] * 5,
        scratch_shapes=[
            pltpu.VMEM(ids.shape, ids.dtype),
            pltpu.VMEM(gates.shape, gates.dtype),
            pltpu.SemaphoreType.DMA((3 + 2 * (width // STEP),)),
        ],
        compiler_params=pltpu.CompilerParams(vmem_limit_bytes=16 * MIB),
        cost_estimate=expert_cost(count, features, width),
        name="own_hidden",
    )(*[in_hbm(v) for v in (tokens, ids, gates, gate, up)])


def own_answer_kernel(experts, hidden_ref, terms_ref, down_hbm, out_ref, down_ref, done):
    features = down_ref.shape[1]
    copies = []
    for i, at in enumerate(range(0, features, 2 * STEP)):
        columns = pl.ds(at, 2 * STEP)
        copies.append(pltpu.make_async_copy(down_hbm.at[:, columns], down_ref.at[:, columns], done.at[i]))
    for copy in copies:
        copy.start()
    weight = row_weights(terms_ref[...], experts, 0)
    hidden = hidden_ref[...]
    for i, at in enumerate(range(0, features, 2 * STEP)):
        copies[i].wait()
        columns = slice(at, at + 2 * STEP)
        out_ref[:, columns] = jnp.dot(hidden, down_ref[:, columns], preferred_element_type=jnp.float32) * weight


def own_answer(hidden, terms, down, experts):
    count, width = hidden.shape
    features = down.shape[1]
    return pl.pallas_call(
        functools.partial(own_answer_kernel, experts),
        out_shape=[jax.ShapeDtypeStruct((count, features), jnp.float32), jax.ShapeDtypeStruct(down.shape, down.dtype)],
        in_specs=[whole()] * 2 + [anywhere()],
        out_specs=[whole()] * 2,
        scratch_shapes=[pltpu.SemaphoreType.DMA((features // (2 * STEP),))],
        compiler_params=pltpu.CompilerParams(vmem_limit_bytes=16 * MIB),
        cost_estimate=expert_cost(count, features, width // 3),
        name="own_answer",
    )(in_vmem(hidden), in_vmem(terms), in_hbm(down))


def nothing(*refs):
    pass


def held(*values, after=()):
    return pl.pallas_call(
        nothing,
        out_shape=[jax.ShapeDtypeStruct(v.shape, v.dtype) for v in values],
        in_specs=[anywhere()] * (len(values) + len(after)),
        out_specs=[anywhere()] * len(values),
        input_output_aliases={i: i for i in range(len(values))},
        compiler_params=pltpu.CompilerParams(vmem_limit_bytes=MIB),
        cost_estimate=pl.CostEstimate(flops=0, bytes_accessed=0, transcendentals=0),
        name="held",
    )(*values, *after)


def append_kernel(rows_ref, terms_ref, out_ref):
    features = rows_ref.shape[1]
    out_ref[:, :features] = rows_ref[...]
    out_ref[:, features:] = terms_ref[...]


def append(rows, terms):
    count, features = rows.shape
    return pl.pallas_call(
        append_kernel,
        out_shape=jax.ShapeDtypeStruct((count, features + terms.shape[1]), rows.dtype),
        in_specs=[whole()] * 2,
        out_specs=whole(),
        compiler_params=pltpu.CompilerParams(vmem_limit_bytes=16 * MIB),
        cost_estimate=pl.CostEstimate(flops=0, bytes_accessed=4 * count * features, transcendentals=0),
        name="append",
    )(in_vmem(rows), in_vmem(terms))


def expert_cost(count, features, width):
    return pl.CostEstimate(
        flops=6 * count * features * width, bytes_accessed=count * features * 4, transcendentals=count * width
    )


def expert_kernel(experts, other, added, after, parts, *refs):
    gate_ref, up_ref, down_ref, rows_ref = refs[:4]
    added_refs = refs[4 : 4 + added * parts]
    out_refs = refs[4 + added * parts + after : -1]
    hidden_ref = refs[-1]
    features, width = gate_ref.shape
    rows = rows_ref[:, :features]
    weight = row_weights(rows_ref[:, features:], experts, other)
    for at in range(0, width, STEP):
        columns = slice(at, at + STEP)
        hidden_ref[:, columns] = hidden_columns(rows, gate_ref, up_ref, columns)
    hidden = hidden_ref[...]
    for at in range(0, features, 2 * STEP):
        columns = slice(at, at + 2 * STEP)
        answer = jnp.dot(hidden, down_ref[:, columns], preferred_element_type=jnp.float32) * weight
        start = 0
        for i, out_ref in enumerate(out_refs):
            part = answer[start : start + out_ref.shape[0]]
            for ref in added_refs[i::parts]:
                part = part + ref[:, columns].astype(jnp.float32)
            out_ref[:, columns] = part.astype(out_ref.dtype)
            start += out_ref.shape[0]


def run_expert(weights, other, experts, rows, kind, *added, parts=1, after=()):
    features, width = weights[0].shape
    count = rows.shape[0]
    operands = [in_vmem(v) for v in (*weights, rows, *(v for group in added for v in group))]
    return pl.pallas_call(
        functools.partial(expert_kernel, experts, other, len(added), len(after), parts),
        out_shape=[jax.ShapeDtypeStruct((count // parts, features), kind)] * parts,
        in_specs=[whole()] * len(operands) + [anywhere()] * len(after),
        out_specs=[whole()] * parts,
        scratch_shapes=[pltpu.VMEM((count, width), jnp.bfloat16)],
        compiler_params=pltpu.CompilerParams(vmem_limit_bytes=16 * MIB),
        cost_estimate=expert_cost(count, features, width),
        name="expert",
    )(*operands, *after)


def sum_kernel(first_ref, second_ref, *refs):
    refs[-1][...] = (first_ref[...].astype(jnp.float32) + second_ref[...].astype(jnp.float32)).astype(refs[-1].dtype)


def sums(first, second, after=()):
    return pl.pallas_call(
        sum_kernel,
        out_shape=jax.ShapeDtypeStruct(first.shape, jnp.bfloat16),
        in_specs=[whole()] * 2 + [anywhere()] * len(after),
        out_specs=whole(),
        compiler_params=pltpu.CompilerParams(vmem_limit_bytes=16 * MIB),
        name="sums",
    )(in_vmem(first), in_vmem(second), *after)


def finish_kernel(whole_ref, upper_ref, lower_ref, out_ref):
    half = upper_ref.shape[0]
    out_ref[:half] = (whole_ref[:half] + upper_ref[...].astype(jnp.float32)).astype(out_ref.dtype)
    out_ref[half:] = (whole_ref[half:] + lower_ref[...].astype(jnp.float32)).astype(out_ref.dtype)


def finish(whole_part, upper, lower):
    return pl.pallas_call(
        finish_kernel,
        out_shape=jax.ShapeDtypeStruct(whole_part.shape, jnp.bfloat16),
        in_specs=[whole()] * 3,
        out_specs=whole(),
        compiler_params=pltpu.CompilerParams(vmem_limit_bytes=16 * MIB),
        name="finish",
    )(in_vmem(whole_part), in_vmem(upper), in_vmem(lower))


def on_four_chips(tokens, expert_ids, gate_values, w_gate, w_up, w_down):
    experts = lax.axis_size("expert")
    weights = (w_gate[0], w_up[0], w_down[0])
    wide, narrow = jnp.float32, jnp.bfloat16
    far = tuple(swap(w, (CORE, CORE)) for w in weights)
    first = swap(tokens, FIRST)
    own, terms, hidden, near_gate, near_up = own_hidden(tokens, expert_ids, gate_values, *weights[:2], experts)
    own, = held(own, after=far[:1])
    second = swap(own, SECOND)
    first = append(first, swap(terms, FIRST))
    third = swap(first, SECOND)

    near_own, near_down = own_answer(hidden, terms, weights[2], experts)
    near = (near_gate, near_up, near_down)
    near_run = functools.partial(run_expert, near, 0, experts)
    far_run = functools.partial(run_expert, far, CORE, experts)
    near_second = near_run(second, wide, after=[near_own])
    sum_second = far_run(second, narrow, near_second)
    back_second = swap(sum_second[0], SECOND)
    near_third = near_run(third, wide, parts=2, after=sum_second)
    sum_third = far_run(third, narrow, near_third, parts=2)
    passed_a, passed_b = swap(sum_third[0], SECOND), swap(sum_third[1], SECOND)
    near_first = near_run(first, wide, parts=2, after=sum_third)
    sum_first = far_run(first, wide, near_first, parts=2)
    sum_own = far_run(own, wide, [near_own], [back_second], after=sum_first)[0]
    back_first_a = swap(sums(sum_first[0], passed_a, after=[sum_own]), FIRST)
    back_first_b = swap(sums(sum_first[1], passed_b, after=[sum_own]), FIRST)
    return finish(sum_own, back_first_a, back_first_b)


def expert_apply(row_block, gate_matrix, up_matrix, down_matrix):
    gate_part = jnp.dot(row_block, gate_matrix, preferred_element_type=jnp.float32)
    up_part = jnp.dot(row_block, up_matrix, preferred_element_type=jnp.float32)
    hidden = (jax.nn.silu(gate_part) * up_part).astype(jnp.bfloat16)
    return jnp.dot(hidden, down_matrix, preferred_element_type=jnp.float32).astype(jnp.bfloat16)


def dispatched(tokens, expert_ids, gate_values, w_gate, w_up, w_down):
    token_count, features = tokens.shape
    topk_width = expert_ids.shape[1]
    experts_all = lax.axis_size("expert")
    pair_ids = expert_ids.reshape(-1)
    pair_rows = jnp.arange(pair_ids.shape[0], dtype=jnp.int32) // topk_width
    other_bound = min(
        token_count,
        ((topk_width - 1) * token_count + experts_all - 3) // (experts_all - 2) * 3 // 2,
    )
    slot_bound = max(token_count * 9 // 16, other_bound)
    one_hot = (pair_ids[:, None] == jnp.arange(experts_all, dtype=jnp.int32)[None, :]).astype(jnp.int32)
    earlier = jnp.cumsum(one_hot, axis=0) - one_hot
    places = pair_ids * slot_bound + jnp.sum(earlier * one_hot, axis=1)
    padded_source = jnp.concatenate([tokens, jnp.zeros((1, features), tokens.dtype)], axis=0)
    slot_table = (
        jnp.full((experts_all * slot_bound,), token_count, jnp.int32).at[places].set(pair_rows, mode="drop")
    )
    outgoing = padded_source[slot_table].reshape(experts_all, slot_bound, features)
    received = lax.all_to_all(outgoing, "expert", split_axis=0, concat_axis=0, tiled=True)
    answer = expert_apply(received.reshape(-1, features), w_gate[0], w_up[0], w_down[0])
    returned = lax.all_to_all(
        answer.reshape(received.shape), "expert", split_axis=0, concat_axis=0, tiled=True
    ).reshape(-1, features)[places]
    weighted = gate_values.reshape(-1)[:, None] * returned.astype(jnp.float32)
    return jnp.sum(weighted.reshape(token_count, topk_width, features), axis=1).astype(jnp.bfloat16)


def solution(mesh):
    placed = (
        P(("dp", "expert"), None),
        P(("dp", "expert"), None),
        P(("dp", "expert"), None),
        P("expert", None, None),
        P("expert", None, None),
        P("expert", None, None),
    )
    body = on_four_chips if mesh.shape["expert"] == 8 else dispatched
    return jax.shard_map(
        body, mesh=mesh, in_specs=placed, out_specs=P(("dp", "expert"), None), check_vma=False
    )
```

```python
import functools

import jax
import jax.numpy as jnp
from jax import lax
from jax.experimental import pallas as pl
from jax.experimental.pallas import tpu as pltpu
from jax.sharding import PartitionSpec as P

CORE, X, Y = 1, 2, 4
FIRST, SECOND = (X, Y), (Y, X)
LANES = 128
STEP = 256
MIB = 2**20


def in_vmem(value):
    return pltpu.with_memory_space_constraint(value, pltpu.VMEM)


def in_hbm(value):
    return pltpu.with_memory_space_constraint(value, pltpu.HBM)


def anywhere():
    return pl.BlockSpec(memory_space=pl.ANY)


def whole():
    return pl.BlockSpec(memory_space=pltpu.VMEM)


def swap(value, offsets):
    size = lax.axis_size("expert")
    return lax.ppermute(value, "expert", [(i, i ^ offsets[i % 2]) for i in range(size)])


def row_terms(ids, gates, experts):
    topk, rows = ids.shape
    line = lax.broadcasted_iota(jnp.int32, (4 * experts, rows), 0)
    expert = line
    for _ in range(3):
        expert = jnp.where(expert >= experts, expert - experts, expert)
    weight = jnp.zeros(line.shape, jnp.float32)
    for k in range(topk):
        weight += jnp.where(expert == ids[k : k + 1, :], gates[k : k + 1, :], 0.0)
    high = weight.astype(jnp.bfloat16).astype(jnp.float32)
    rest = weight - high
    middle = rest.astype(jnp.bfloat16).astype(jnp.float32)
    low = rest - middle
    terms = jnp.where(line < experts, high, jnp.where(line < 2 * experts, middle, low))
    return jnp.where(line < 3 * experts, terms, 0.0).astype(jnp.bfloat16)


def row_weights(terms, experts, other):
    count = terms.shape[1]
    line = lax.broadcasted_iota(jnp.int32, terms.shape, 0)
    own = lax.axis_index("expert") ^ other
    chosen = (line == own) | (line == own + experts) | (line == own + 2 * experts)
    weights = jnp.sum(jnp.where(chosen, terms.astype(jnp.float32), 0.0), axis=0, keepdims=True)
    square = (count, count)
    same = lax.broadcasted_iota(jnp.int32, square, 0) == lax.broadcasted_iota(jnp.int32, square, 1)
    return jnp.sum(jnp.where(same, jnp.broadcast_to(weights, square), 0.0), axis=1, keepdims=True)


def put_blocks(rows, terms, out_ref):
    count, features = rows.shape
    for i in range(features // LANES):
        out_ref[i * count : (i + 1) * count, :] = rows[:, i * LANES : (i + 1) * LANES]
    out_ref[features // LANES * count :, :] = terms


def rows_of(blocks_ref, features):
    count = LANES
    return jnp.concatenate([blocks_ref[i * count : (i + 1) * count, :] for i in range(features // LANES)], axis=1)


def terms_of(blocks_ref, features):
    return blocks_ref[features:, :]


def hidden_columns(rows, gate_ref, up_ref, columns):
    gate = jnp.dot(rows, gate_ref[:, columns], preferred_element_type=jnp.float32)
    up = jnp.dot(rows, up_ref[:, columns], preferred_element_type=jnp.float32)
    return (gate / (1.0 + jnp.exp(-gate)) * up).astype(jnp.bfloat16)


def own_hidden_kernel(
    experts, tokens_hbm, ids_hbm, gates_hbm, gate_hbm, up_hbm, blocks_ref, terms_ref, hidden_ref, gate_ref, up_ref, ids, gates, tokens, done
):
    width = gate_ref.shape[1]
    pairs = [(ids_hbm, ids), (gates_hbm, gates), (tokens_hbm, tokens)]
    for at in range(0, width, STEP):
        columns = pl.ds(at, STEP)
        pairs.append((gate_hbm.at[:, columns], gate_ref.at[:, columns]))
        pairs.append((up_hbm.at[:, columns], up_ref.at[:, columns]))
    copies = [pltpu.make_async_copy(a, b, done.at[i]) for i, (a, b) in enumerate(pairs)]
    for copy in copies:
        copy.start()
    copies[0].wait()
    copies[1].wait()
    terms = row_terms(ids, gates, experts)
    terms_ref[...] = terms
    copies[2].wait()
    rows = tokens[...]
    put_blocks(rows, terms, blocks_ref)
    waits = iter(copies[3:])
    for at in range(0, width, STEP):
        next(waits).wait()
        next(waits).wait()
        columns = slice(at, at + STEP)
        hidden_ref[:, columns] = hidden_columns(rows, gate_ref, up_ref, columns)


def own_hidden(tokens, ids, gates, gate, up, experts):
    count, features = tokens.shape
    width = gate.shape[1]
    ids, gates = ids.T, gates.T
    return pl.pallas_call(
        functools.partial(own_hidden_kernel, experts),
        out_shape=[
            jax.ShapeDtypeStruct((features + 4 * experts, LANES), tokens.dtype),
            jax.ShapeDtypeStruct((4 * experts, LANES), tokens.dtype),
            jax.ShapeDtypeStruct((count, width), tokens.dtype),
            jax.ShapeDtypeStruct(gate.shape, gate.dtype),
            jax.ShapeDtypeStruct(up.shape, up.dtype),
        ],
        in_specs=[anywhere()] * 5,
        out_specs=[whole()] * 5,
        scratch_shapes=[
            pltpu.VMEM(ids.shape, ids.dtype),
            pltpu.VMEM(gates.shape, gates.dtype),
            pltpu.VMEM(tokens.shape, tokens.dtype),
            pltpu.SemaphoreType.DMA((3 + 2 * (width // STEP),)),
        ],
        compiler_params=pltpu.CompilerParams(vmem_limit_bytes=16 * MIB),
        cost_estimate=expert_cost(count, features, width),
        name="own_hidden",
    )(*[in_hbm(v) for v in (tokens, ids, gates, gate, up)])


def own_answer_kernel(experts, hidden_ref, terms_ref, down_hbm, out_ref, down_ref, done):
    features = down_ref.shape[1]
    copies = []
    for i, at in enumerate(range(0, features, 2 * STEP)):
        columns = pl.ds(at, 2 * STEP)
        copies.append(pltpu.make_async_copy(down_hbm.at[:, columns], down_ref.at[:, columns], done.at[i]))
    for copy in copies:
        copy.start()
    weight = row_weights(terms_ref[...], experts, 0)
    hidden = hidden_ref[...]
    for i, at in enumerate(range(0, features, 2 * STEP)):
        copies[i].wait()
        columns = slice(at, at + 2 * STEP)
        out_ref[:, columns] = jnp.dot(hidden, down_ref[:, columns], preferred_element_type=jnp.float32) * weight


def own_answer(hidden, terms, down, experts):
    count, width = hidden.shape
    features = down.shape[1]
    return pl.pallas_call(
        functools.partial(own_answer_kernel, experts),
        out_shape=[jax.ShapeDtypeStruct((count, features), jnp.float32), jax.ShapeDtypeStruct(down.shape, down.dtype)],
        in_specs=[whole()] * 2 + [anywhere()],
        out_specs=[whole()] * 2,
        scratch_shapes=[pltpu.SemaphoreType.DMA((features // (2 * STEP),))],
        compiler_params=pltpu.CompilerParams(vmem_limit_bytes=16 * MIB),
        cost_estimate=expert_cost(count, features, width // 3),
        name="own_answer",
    )(in_vmem(hidden), in_vmem(terms), in_hbm(down))


def nothing(*refs):
    pass


def held(*values, after=()):
    return pl.pallas_call(
        nothing,
        out_shape=[jax.ShapeDtypeStruct(v.shape, v.dtype) for v in values],
        in_specs=[anywhere()] * (len(values) + len(after)),
        out_specs=[anywhere()] * len(values),
        input_output_aliases={i: i for i in range(len(values))},
        compiler_params=pltpu.CompilerParams(vmem_limit_bytes=MIB),
        cost_estimate=pl.CostEstimate(flops=0, bytes_accessed=0, transcendentals=0),
        name="held",
    )(*values, *after)


def append_kernel(rows_ref, terms_ref, *refs):
    put_blocks(rows_ref[...], terms_ref[...], refs[-1])


def append(rows, terms, *after):
    count, features = rows.shape
    return pl.pallas_call(
        append_kernel,
        out_shape=jax.ShapeDtypeStruct((features + terms.shape[0], LANES), rows.dtype),
        in_specs=[whole()] * 2 + [anywhere()] * len(after),
        out_specs=whole(),
        compiler_params=pltpu.CompilerParams(vmem_limit_bytes=16 * MIB),
        cost_estimate=pl.CostEstimate(flops=0, bytes_accessed=4 * count * features, transcendentals=0),
        name="append",
    )(in_vmem(rows), in_vmem(terms), *after)


def expert_cost(count, features, width):
    return pl.CostEstimate(
        flops=6 * count * features * width, bytes_accessed=count * features * 4, transcendentals=count * width
    )


def expert_kernel(experts, other, added, after, parts, *refs):
    gate_ref, up_ref, down_ref, blocks_ref = refs[:4]
    added_refs = refs[4 : 4 + added * parts]
    out_refs = refs[4 + added * parts + after : -1]
    hidden_ref = refs[-1]
    features, width = gate_ref.shape
    rows = rows_of(blocks_ref, features)
    weight = row_weights(terms_of(blocks_ref, features), experts, other)
    for at in range(0, width, STEP):
        columns = slice(at, at + STEP)
        hidden_ref[:, columns] = hidden_columns(rows, gate_ref, up_ref, columns)
    hidden = hidden_ref[...]
    for at in range(0, features, 2 * STEP):
        columns = slice(at, at + 2 * STEP)
        answer = jnp.dot(hidden, down_ref[:, columns], preferred_element_type=jnp.float32) * weight
        start = 0
        for i, out_ref in enumerate(out_refs):
            part = answer[start : start + out_ref.shape[0]]
            for ref in added_refs[i::parts]:
                part = part + ref[:, columns].astype(jnp.float32)
            out_ref[:, columns] = part.astype(out_ref.dtype)
            start += out_ref.shape[0]


def run_expert(weights, other, experts, blocks, kind, *added, parts=1, after=()):
    features, width = weights[0].shape
    count = LANES
    operands = [in_vmem(v) for v in (*weights, blocks, *(v for group in added for v in group))]
    return pl.pallas_call(
        functools.partial(expert_kernel, experts, other, len(added), len(after), parts),
        out_shape=[jax.ShapeDtypeStruct((count // parts, features), kind)] * parts,
        in_specs=[whole()] * len(operands) + [anywhere()] * len(after),
        out_specs=[whole()] * parts,
        scratch_shapes=[pltpu.VMEM((count, width), jnp.bfloat16)],
        compiler_params=pltpu.CompilerParams(vmem_limit_bytes=16 * MIB),
        cost_estimate=expert_cost(count, features, width),
        name="expert",
    )(*operands, *after)


def sum_kernel(first_ref, second_ref, *refs):
    refs[-1][...] = (first_ref[...].astype(jnp.float32) + second_ref[...].astype(jnp.float32)).astype(refs[-1].dtype)


def sums(first, second, after=()):
    return pl.pallas_call(
        sum_kernel,
        out_shape=jax.ShapeDtypeStruct(first.shape, jnp.bfloat16),
        in_specs=[whole()] * 2 + [anywhere()] * len(after),
        out_specs=whole(),
        compiler_params=pltpu.CompilerParams(vmem_limit_bytes=16 * MIB),
        name="sums",
    )(in_vmem(first), in_vmem(second), *after)


def finish_kernel(whole_ref, upper_ref, lower_ref, out_ref):
    half = upper_ref.shape[0]
    out_ref[:half] = (whole_ref[:half] + upper_ref[...].astype(jnp.float32)).astype(out_ref.dtype)
    out_ref[half:] = (whole_ref[half:] + lower_ref[...].astype(jnp.float32)).astype(out_ref.dtype)


def finish(whole_part, upper, lower):
    return pl.pallas_call(
        finish_kernel,
        out_shape=jax.ShapeDtypeStruct(whole_part.shape, jnp.bfloat16),
        in_specs=[whole()] * 3,
        out_specs=whole(),
        compiler_params=pltpu.CompilerParams(vmem_limit_bytes=16 * MIB),
        name="finish",
    )(in_vmem(whole_part), in_vmem(upper), in_vmem(lower))


def on_four_chips(tokens, expert_ids, gate_values, w_gate, w_up, w_down):
    experts = lax.axis_size("expert")
    weights = (w_gate[0], w_up[0], w_down[0])
    wide, narrow = jnp.float32, jnp.bfloat16
    far = tuple(swap(w, (CORE, CORE)) for w in weights)
    first = swap(tokens, FIRST)
    own, terms, hidden, near_gate, near_up = own_hidden(tokens, expert_ids, gate_values, *weights[:2], experts)
    own, = held(own, after=far[:1])
    second = swap(own, SECOND)
    near_own, near_down = own_answer(hidden, terms, weights[2], experts)
    first = append(first, swap(terms, FIRST), near_own)
    third = swap(first, SECOND)

    near = (near_gate, near_up, near_down)
    near_run = functools.partial(run_expert, near, 0, experts)
    far_run = functools.partial(run_expert, far, CORE, experts)
    near_first = near_run(first, wide, parts=2, after=[near_own])
    near_second = near_run(second, wide, after=near_first)
    sum_second = far_run(second, narrow, near_second)
    back_second = swap(sum_second[0], SECOND)
    near_third = near_run(third, wide, parts=2, after=sum_second)
    sum_third = far_run(third, narrow, near_third, parts=2)
    passed_a, passed_b = swap(sum_third[0], SECOND), swap(sum_third[1], SECOND)
    sum_first = far_run(first, wide, near_first, parts=2, after=sum_third)
    sum_own = far_run(own, wide, [near_own], [back_second], after=sum_first)[0]
    back_first_a = swap(sums(sum_first[0], passed_a, after=[sum_own]), FIRST)
    back_first_b = swap(sums(sum_first[1], passed_b, after=[sum_own]), FIRST)
    return finish(sum_own, back_first_a, back_first_b)


def expert_apply(row_block, gate_matrix, up_matrix, down_matrix):
    gate_part = jnp.dot(row_block, gate_matrix, preferred_element_type=jnp.float32)
    up_part = jnp.dot(row_block, up_matrix, preferred_element_type=jnp.float32)
    hidden = (jax.nn.silu(gate_part) * up_part).astype(jnp.bfloat16)
    return jnp.dot(hidden, down_matrix, preferred_element_type=jnp.float32).astype(jnp.bfloat16)


def dispatched(tokens, expert_ids, gate_values, w_gate, w_up, w_down):
    token_count, features = tokens.shape
    topk_width = expert_ids.shape[1]
    experts_all = lax.axis_size("expert")
    pair_ids = expert_ids.reshape(-1)
    pair_rows = jnp.arange(pair_ids.shape[0], dtype=jnp.int32) // topk_width
    other_bound = min(
        token_count,
        ((topk_width - 1) * token_count + experts_all - 3) // (experts_all - 2) * 3 // 2,
    )
    slot_bound = max(token_count * 9 // 16, other_bound)
    one_hot = (pair_ids[:, None] == jnp.arange(experts_all, dtype=jnp.int32)[None, :]).astype(jnp.int32)
    earlier = jnp.cumsum(one_hot, axis=0) - one_hot
    places = pair_ids * slot_bound + jnp.sum(earlier * one_hot, axis=1)
    padded_source = jnp.concatenate([tokens, jnp.zeros((1, features), tokens.dtype)], axis=0)
    slot_table = (
        jnp.full((experts_all * slot_bound,), token_count, jnp.int32).at[places].set(pair_rows, mode="drop")
    )
    outgoing = padded_source[slot_table].reshape(experts_all, slot_bound, features)
    received = lax.all_to_all(outgoing, "expert", split_axis=0, concat_axis=0, tiled=True)
    answer = expert_apply(received.reshape(-1, features), w_gate[0], w_up[0], w_down[0])
    returned = lax.all_to_all(
        answer.reshape(received.shape), "expert", split_axis=0, concat_axis=0, tiled=True
    ).reshape(-1, features)[places]
    weighted = gate_values.reshape(-1)[:, None] * returned.astype(jnp.float32)
    return jnp.sum(weighted.reshape(token_count, topk_width, features), axis=1).astype(jnp.bfloat16)


def solution(mesh):
    placed = (
        P(("dp", "expert"), None),
        P(("dp", "expert"), None),
        P(("dp", "expert"), None),
        P("expert", None, None),
        P("expert", None, None),
        P("expert", None, None),
    )
    def body(tokens, *others):
        here = mesh.shape["expert"] == 8 and tokens.shape[0] == LANES
        return (on_four_chips if here else dispatched)(tokens, *others)

    return jax.shard_map(
        body, mesh=mesh, in_specs=placed, out_specs=P(("dp", "expert"), None), check_vma=False
    )
```

```python
import functools

import jax
import jax.numpy as jnp
from jax import lax
from jax.experimental import pallas as pl
from jax.experimental.pallas import tpu as pltpu
from jax.sharding import PartitionSpec as P

CORE, X, Y = 1, 2, 4
FIRST, SECOND = (X, Y), (Y, X)
LANES = 128
STEP = 256
MIB = 2**20


def in_vmem(value):
    return pltpu.with_memory_space_constraint(value, pltpu.VMEM)


def in_hbm(value):
    return pltpu.with_memory_space_constraint(value, pltpu.HBM)


def anywhere():
    return pl.BlockSpec(memory_space=pl.ANY)


def whole():
    return pl.BlockSpec(memory_space=pltpu.VMEM)


def swap(value, offsets):
    size = lax.axis_size("expert")
    return lax.ppermute(value, "expert", [(i, i ^ offsets[i % 2]) for i in range(size)])


def row_terms(ids, gates, experts):
    topk, rows = ids.shape
    line = lax.broadcasted_iota(jnp.int32, (4 * experts, rows), 0)
    expert = line
    for _ in range(3):
        expert = jnp.where(expert >= experts, expert - experts, expert)
    weight = jnp.zeros(line.shape, jnp.float32)
    for k in range(topk):
        weight += jnp.where(expert == ids[k : k + 1, :], gates[k : k + 1, :], 0.0)
    high = weight.astype(jnp.bfloat16).astype(jnp.float32)
    rest = weight - high
    middle = rest.astype(jnp.bfloat16).astype(jnp.float32)
    low = rest - middle
    terms = jnp.where(line < experts, high, jnp.where(line < 2 * experts, middle, low))
    return jnp.where(line < 3 * experts, terms, 0.0).astype(jnp.bfloat16)


def row_weights(terms, experts, other):
    count = terms.shape[1]
    line = lax.broadcasted_iota(jnp.int32, terms.shape, 0)
    own = lax.axis_index("expert") ^ other
    chosen = (line == own) | (line == own + experts) | (line == own + 2 * experts)
    weights = jnp.sum(jnp.where(chosen, terms.astype(jnp.float32), 0.0), axis=0, keepdims=True)
    square = (count, count)
    same = lax.broadcasted_iota(jnp.int32, square, 0) == lax.broadcasted_iota(jnp.int32, square, 1)
    return jnp.sum(jnp.where(same, jnp.broadcast_to(weights, square), 0.0), axis=1, keepdims=True)


def put_blocks(rows, terms, out_ref):
    count, features = rows.shape
    for i in range(features // LANES):
        out_ref[i * count : (i + 1) * count, :] = rows[:, i * LANES : (i + 1) * LANES]
    out_ref[features // LANES * count :, :] = terms


def rows_of(blocks_ref, features):
    count = LANES
    return jnp.concatenate([blocks_ref[i * count : (i + 1) * count, :] for i in range(features // LANES)], axis=1)


def terms_of(blocks_ref, features):
    return blocks_ref[features:, :]


def hidden_columns(rows, gate_ref, up_ref, columns):
    gate = jnp.dot(rows, gate_ref[:, columns], preferred_element_type=jnp.float32)
    up = jnp.dot(rows, up_ref[:, columns], preferred_element_type=jnp.float32)
    return (gate / (1.0 + jnp.exp(-gate)) * up).astype(jnp.bfloat16)


def own_hidden_kernel(
    experts, tokens_hbm, ids_hbm, gates_hbm, gate_hbm, up_hbm, blocks_ref, terms_ref, hidden_ref, gate_ref, up_ref, ids, gates, tokens, done
):
    width = gate_ref.shape[1]
    pairs = [(ids_hbm, ids), (gates_hbm, gates), (tokens_hbm, tokens)]
    for at in range(0, width, STEP):
        columns = pl.ds(at, STEP)
        pairs.append((gate_hbm.at[:, columns], gate_ref.at[:, columns]))
        pairs.append((up_hbm.at[:, columns], up_ref.at[:, columns]))
    copies = [pltpu.make_async_copy(a, b, done.at[i]) for i, (a, b) in enumerate(pairs)]
    for copy in copies:
        copy.start()
    copies[0].wait()
    copies[1].wait()
    terms = row_terms(ids, gates, experts)
    terms_ref[...] = terms
    copies[2].wait()
    rows = tokens[...]
    put_blocks(rows, terms, blocks_ref)
    waits = iter(copies[3:])
    for at in range(0, width, STEP):
        next(waits).wait()
        next(waits).wait()
        columns = slice(at, at + STEP)
        hidden_ref[:, columns] = hidden_columns(rows, gate_ref, up_ref, columns)


def own_hidden(tokens, ids, gates, gate, up, experts):
    count, features = tokens.shape
    width = gate.shape[1]
    ids, gates = ids.T, gates.T
    return pl.pallas_call(
        functools.partial(own_hidden_kernel, experts),
        out_shape=[
            jax.ShapeDtypeStruct((features + 4 * experts, LANES), tokens.dtype),
            jax.ShapeDtypeStruct((4 * experts, LANES), tokens.dtype),
            jax.ShapeDtypeStruct((count, width), tokens.dtype),
            jax.ShapeDtypeStruct(gate.shape, gate.dtype),
            jax.ShapeDtypeStruct(up.shape, up.dtype),
        ],
        in_specs=[anywhere()] * 5,
        out_specs=[whole()] * 5,
        scratch_shapes=[
            pltpu.VMEM(ids.shape, ids.dtype),
            pltpu.VMEM(gates.shape, gates.dtype),
            pltpu.VMEM(tokens.shape, tokens.dtype),
            pltpu.SemaphoreType.DMA((3 + 2 * (width // STEP),)),
        ],
        compiler_params=pltpu.CompilerParams(vmem_limit_bytes=16 * MIB),
        cost_estimate=expert_cost(36 * count, features, width),
        name="own_hidden",
    )(*[in_hbm(v) for v in (tokens, ids, gates, gate, up)])


def own_answer_kernel(experts, hidden_ref, terms_ref, down_hbm, out_ref, down_ref, done):
    features = down_ref.shape[1]
    copies = []
    for i, at in enumerate(range(0, features, 2 * STEP)):
        columns = pl.ds(at, 2 * STEP)
        copies.append(pltpu.make_async_copy(down_hbm.at[:, columns], down_ref.at[:, columns], done.at[i]))
    for copy in copies:
        copy.start()
    weight = row_weights(terms_ref[...], experts, 0)
    hidden = hidden_ref[...]
    for i, at in enumerate(range(0, features, 2 * STEP)):
        copies[i].wait()
        columns = slice(at, at + 2 * STEP)
        out_ref[:, columns] = jnp.dot(hidden, down_ref[:, columns], preferred_element_type=jnp.float32) * weight


def own_answer(hidden, terms, down, experts):
    count, width = hidden.shape
    features = down.shape[1]
    return pl.pallas_call(
        functools.partial(own_answer_kernel, experts),
        out_shape=[jax.ShapeDtypeStruct((count, features), jnp.float32), jax.ShapeDtypeStruct(down.shape, down.dtype)],
        in_specs=[whole()] * 2 + [anywhere()],
        out_specs=[whole()] * 2,
        scratch_shapes=[pltpu.SemaphoreType.DMA((features // (2 * STEP),))],
        compiler_params=pltpu.CompilerParams(vmem_limit_bytes=16 * MIB),
        cost_estimate=expert_cost(count, features, width // 3),
        name="own_answer",
    )(in_vmem(hidden), in_vmem(terms), in_hbm(down))


def nothing(*refs):
    pass


def held(*values, after=()):
    return pl.pallas_call(
        nothing,
        out_shape=[jax.ShapeDtypeStruct(v.shape, v.dtype) for v in values],
        in_specs=[anywhere()] * (len(values) + len(after)),
        out_specs=[anywhere()] * len(values),
        input_output_aliases={i: i for i in range(len(values))},
        compiler_params=pltpu.CompilerParams(vmem_limit_bytes=MIB),
        cost_estimate=pl.CostEstimate(flops=0, bytes_accessed=0, transcendentals=0),
        name="held",
    )(*values, *after)


def append_kernel(rows_ref, terms_ref, *refs):
    put_blocks(rows_ref[...], terms_ref[...], refs[-1])


def append(rows, terms, *after):
    count, features = rows.shape
    return pl.pallas_call(
        append_kernel,
        out_shape=jax.ShapeDtypeStruct((features + terms.shape[0], LANES), rows.dtype),
        in_specs=[whole()] * 2 + [anywhere()] * len(after),
        out_specs=whole(),
        compiler_params=pltpu.CompilerParams(vmem_limit_bytes=16 * MIB),
        cost_estimate=pl.CostEstimate(flops=0, bytes_accessed=4 * count * features, transcendentals=0),
        name="append",
    )(in_vmem(rows), in_vmem(terms), *after)


def expert_cost(count, features, width):
    return pl.CostEstimate(
        flops=6 * count * features * width, bytes_accessed=count * features * 4, transcendentals=count * width
    )


def expert_kernel(experts, other, added, after, parts, *refs):
    gate_ref, up_ref, down_ref, blocks_ref = refs[:4]
    added_refs = refs[4 : 4 + added * parts]
    out_refs = refs[4 + added * parts + after : -1]
    hidden_ref = refs[-1]
    features, width = gate_ref.shape
    rows = rows_of(blocks_ref, features)
    weight = row_weights(terms_of(blocks_ref, features), experts, other)
    for at in range(0, width, STEP):
        columns = slice(at, at + STEP)
        hidden_ref[:, columns] = hidden_columns(rows, gate_ref, up_ref, columns)
    hidden = hidden_ref[...]
    for at in range(0, features, 2 * STEP):
        columns = slice(at, at + 2 * STEP)
        answer = jnp.dot(hidden, down_ref[:, columns], preferred_element_type=jnp.float32) * weight
        start = 0
        for i, out_ref in enumerate(out_refs):
            part = answer[start : start + out_ref.shape[0]]
            for ref in added_refs[i::parts]:
                part = part + ref[:, columns].astype(jnp.float32)
            out_ref[:, columns] = part.astype(out_ref.dtype)
            start += out_ref.shape[0]


def run_expert(weights, other, experts, blocks, kind, *added, parts=1, after=()):
    features, width = weights[0].shape
    count = LANES
    operands = [in_vmem(v) for v in (*weights, blocks, *(v for group in added for v in group))]
    return pl.pallas_call(
        functools.partial(expert_kernel, experts, other, len(added), len(after), parts),
        out_shape=[jax.ShapeDtypeStruct((count // parts, features), kind)] * parts,
        in_specs=[whole()] * len(operands) + [anywhere()] * len(after),
        out_specs=[whole()] * parts,
        scratch_shapes=[pltpu.VMEM((count, width), jnp.bfloat16)],
        compiler_params=pltpu.CompilerParams(vmem_limit_bytes=16 * MIB),
        cost_estimate=expert_cost(count, features, width),
        name="expert",
    )(*operands, *after)


def sum_kernel(first_ref, second_ref, *refs):
    refs[-1][...] = (first_ref[...].astype(jnp.float32) + second_ref[...].astype(jnp.float32)).astype(refs[-1].dtype)


def sums(first, second, after=()):
    return pl.pallas_call(
        sum_kernel,
        out_shape=jax.ShapeDtypeStruct(first.shape, jnp.bfloat16),
        in_specs=[whole()] * 2 + [anywhere()] * len(after),
        out_specs=whole(),
        compiler_params=pltpu.CompilerParams(vmem_limit_bytes=16 * MIB),
        name="sums",
    )(in_vmem(first), in_vmem(second), *after)


def finish_kernel(whole_ref, upper_ref, lower_ref, out_ref):
    half = upper_ref.shape[0]
    out_ref[:half] = (whole_ref[:half] + upper_ref[...].astype(jnp.float32)).astype(out_ref.dtype)
    out_ref[half:] = (whole_ref[half:] + lower_ref[...].astype(jnp.float32)).astype(out_ref.dtype)


def finish(whole_part, upper, lower):
    return pl.pallas_call(
        finish_kernel,
        out_shape=jax.ShapeDtypeStruct(whole_part.shape, jnp.bfloat16),
        in_specs=[whole()] * 3,
        out_specs=whole(),
        compiler_params=pltpu.CompilerParams(vmem_limit_bytes=16 * MIB),
        name="finish",
    )(in_vmem(whole_part), in_vmem(upper), in_vmem(lower))


def on_four_chips(tokens, expert_ids, gate_values, w_gate, w_up, w_down):
    experts = lax.axis_size("expert")
    weights = (w_gate[0], w_up[0], w_down[0])
    wide, narrow = jnp.float32, jnp.bfloat16
    far = tuple(swap(w, (CORE, CORE)) for w in weights)
    first = swap(tokens, FIRST)
    own, terms, hidden, near_gate, near_up = own_hidden(tokens, expert_ids, gate_values, *weights[:2], experts)
    second = swap(own, SECOND)
    terms, = held(terms, after=far[:1])
    near_own, near_down = own_answer(hidden, terms, weights[2], experts)
    first = append(first, swap(terms, FIRST), near_own)
    third = swap(first, SECOND)

    near = (near_gate, near_up, near_down)
    near_run = functools.partial(run_expert, near, 0, experts)
    far_run = functools.partial(run_expert, far, CORE, experts)
    near_first = near_run(first, wide, parts=2, after=[near_own])
    near_second = near_run(second, wide, after=near_first)
    sum_second = far_run(second, narrow, near_second)
    back_second = swap(sum_second[0], SECOND)
    near_third = near_run(third, wide, parts=2, after=sum_second)
    sum_third = far_run(third, narrow, near_third, parts=2)
    passed_a, passed_b = swap(sum_third[0], SECOND), swap(sum_third[1], SECOND)
    sum_first = far_run(first, wide, near_first, parts=2, after=sum_third)
    sum_own = far_run(own, wide, [near_own], [back_second], after=sum_first)[0]
    back_first_a = swap(sums(sum_first[0], passed_a, after=[sum_own]), FIRST)
    back_first_b = swap(sums(sum_first[1], passed_b, after=[sum_own]), FIRST)
    return finish(sum_own, back_first_a, back_first_b)


def expert_apply(row_block, gate_matrix, up_matrix, down_matrix):
    gate_part = jnp.dot(row_block, gate_matrix, preferred_element_type=jnp.float32)
    up_part = jnp.dot(row_block, up_matrix, preferred_element_type=jnp.float32)
    hidden = (jax.nn.silu(gate_part) * up_part).astype(jnp.bfloat16)
    return jnp.dot(hidden, down_matrix, preferred_element_type=jnp.float32).astype(jnp.bfloat16)


def dispatched(tokens, expert_ids, gate_values, w_gate, w_up, w_down):
    token_count, features = tokens.shape
    topk_width = expert_ids.shape[1]
    experts_all = lax.axis_size("expert")
    pair_ids = expert_ids.reshape(-1)
    pair_rows = jnp.arange(pair_ids.shape[0], dtype=jnp.int32) // topk_width
    other_bound = min(
        token_count,
        ((topk_width - 1) * token_count + experts_all - 3) // (experts_all - 2) * 3 // 2,
    )
    slot_bound = max(token_count * 9 // 16, other_bound)
    one_hot = (pair_ids[:, None] == jnp.arange(experts_all, dtype=jnp.int32)[None, :]).astype(jnp.int32)
    earlier = jnp.cumsum(one_hot, axis=0) - one_hot
    places = pair_ids * slot_bound + jnp.sum(earlier * one_hot, axis=1)
    padded_source = jnp.concatenate([tokens, jnp.zeros((1, features), tokens.dtype)], axis=0)
    slot_table = (
        jnp.full((experts_all * slot_bound,), token_count, jnp.int32).at[places].set(pair_rows, mode="drop")
    )
    outgoing = padded_source[slot_table].reshape(experts_all, slot_bound, features)
    received = lax.all_to_all(outgoing, "expert", split_axis=0, concat_axis=0, tiled=True)
    answer = expert_apply(received.reshape(-1, features), w_gate[0], w_up[0], w_down[0])
    returned = lax.all_to_all(
        answer.reshape(received.shape), "expert", split_axis=0, concat_axis=0, tiled=True
    ).reshape(-1, features)[places]
    weighted = gate_values.reshape(-1)[:, None] * returned.astype(jnp.float32)
    return jnp.sum(weighted.reshape(token_count, topk_width, features), axis=1).astype(jnp.bfloat16)


def solution(mesh):
    placed = (
        P(("dp", "expert"), None),
        P(("dp", "expert"), None),
        P(("dp", "expert"), None),
        P("expert", None, None),
        P("expert", None, None),
        P("expert", None, None),
    )
    def body(tokens, *others):
        here = mesh.shape["expert"] == 8 and tokens.shape[0] == LANES
        return (on_four_chips if here else dispatched)(tokens, *others)

    return jax.shard_map(
        body, mesh=mesh, in_specs=placed, out_specs=P(("dp", "expert"), None), check_vma=False
    )
```

```python
import functools

import jax
import jax.numpy as jnp
from jax import lax
from jax.experimental import pallas as pl
from jax.experimental.pallas import tpu as pltpu
from jax.sharding import PartitionSpec as P

CORE, X, Y = 1, 2, 4
FIRST, SECOND = (X, Y), (Y, X)
LANES = 128
STEP = 256
MIB = 2**20


def in_vmem(value):
    return pltpu.with_memory_space_constraint(value, pltpu.VMEM)


def in_hbm(value):
    return pltpu.with_memory_space_constraint(value, pltpu.HBM)


def anywhere():
    return pl.BlockSpec(memory_space=pl.ANY)


def whole():
    return pl.BlockSpec(memory_space=pltpu.VMEM)


def swap(value, offsets):
    size = lax.axis_size("expert")
    return lax.ppermute(value, "expert", [(i, i ^ offsets[i % 2]) for i in range(size)])


def row_terms(ids, gates, experts):
    topk, rows = ids.shape
    line = lax.broadcasted_iota(jnp.int32, (4 * experts, rows), 0)
    expert = line
    for _ in range(3):
        expert = jnp.where(expert >= experts, expert - experts, expert)
    weight = jnp.zeros(line.shape, jnp.float32)
    for k in range(topk):
        weight += jnp.where(expert == ids[k : k + 1, :], gates[k : k + 1, :], 0.0)
    high = weight.astype(jnp.bfloat16).astype(jnp.float32)
    rest = weight - high
    middle = rest.astype(jnp.bfloat16).astype(jnp.float32)
    low = rest - middle
    terms = jnp.where(line < experts, high, jnp.where(line < 2 * experts, middle, low))
    return jnp.where(line < 3 * experts, terms, 0.0).astype(jnp.bfloat16)


def row_weights(terms, experts, other):
    count = terms.shape[1]
    line = lax.broadcasted_iota(jnp.int32, terms.shape, 0)
    own = lax.axis_index("expert") ^ other
    chosen = (line == own) | (line == own + experts) | (line == own + 2 * experts)
    weights = jnp.sum(jnp.where(chosen, terms.astype(jnp.float32), 0.0), axis=0, keepdims=True)
    square = (count, count)
    same = lax.broadcasted_iota(jnp.int32, square, 0) == lax.broadcasted_iota(jnp.int32, square, 1)
    return jnp.sum(jnp.where(same, jnp.broadcast_to(weights, square), 0.0), axis=1, keepdims=True)


def put_blocks(rows, terms, out_ref):
    count, features = rows.shape
    for i in range(features // LANES):
        out_ref[i * count : (i + 1) * count, :] = rows[:, i * LANES : (i + 1) * LANES]
    out_ref[features // LANES * count :, :] = terms


def rows_of(blocks_ref, features):
    count = LANES
    return jnp.concatenate([blocks_ref[i * count : (i + 1) * count, :] for i in range(features // LANES)], axis=1)


def terms_of(blocks_ref, features):
    return blocks_ref[features:, :]


def hidden_columns(rows, gate_ref, up_ref, columns):
    gate = jnp.dot(rows, gate_ref[:, columns], preferred_element_type=jnp.float32)
    up = jnp.dot(rows, up_ref[:, columns], preferred_element_type=jnp.float32)
    return (gate / (1.0 + jnp.exp(-gate)) * up).astype(jnp.bfloat16)


def own_hidden_kernel(
    experts, tokens_hbm, ids_hbm, gates_hbm, gate_hbm, up_hbm, blocks_ref, terms_ref, hidden_ref, gate_ref, up_ref, ids, gates, tokens, done
):
    width = gate_ref.shape[1]
    pairs = [(ids_hbm, ids), (gates_hbm, gates), (tokens_hbm, tokens)]
    for at in range(0, width, STEP):
        columns = pl.ds(at, STEP)
        pairs.append((gate_hbm.at[:, columns], gate_ref.at[:, columns]))
        pairs.append((up_hbm.at[:, columns], up_ref.at[:, columns]))
    copies = [pltpu.make_async_copy(a, b, done.at[i]) for i, (a, b) in enumerate(pairs)]
    for copy in copies:
        copy.start()
    copies[0].wait()
    copies[1].wait()
    terms = row_terms(ids, gates, experts)
    terms_ref[...] = terms
    copies[2].wait()
    rows = tokens[...]
    put_blocks(rows, terms, blocks_ref)
    waits = iter(copies[3:])
    for at in range(0, width, STEP):
        next(waits).wait()
        next(waits).wait()
        columns = slice(at, at + STEP)
        hidden_ref[:, columns] = hidden_columns(rows, gate_ref, up_ref, columns)


def own_hidden(tokens, ids, gates, gate, up, experts):
    count, features = tokens.shape
    width = gate.shape[1]
    ids, gates = ids.T, gates.T
    return pl.pallas_call(
        functools.partial(own_hidden_kernel, experts),
        out_shape=[
            jax.ShapeDtypeStruct((features + 4 * experts, LANES), tokens.dtype),
            jax.ShapeDtypeStruct((4 * experts, LANES), tokens.dtype),
            jax.ShapeDtypeStruct((count, width), tokens.dtype),
            jax.ShapeDtypeStruct(gate.shape, gate.dtype),
            jax.ShapeDtypeStruct(up.shape, up.dtype),
        ],
        in_specs=[anywhere()] * 5,
        out_specs=[whole()] * 5,
        scratch_shapes=[
            pltpu.VMEM(ids.shape, ids.dtype),
            pltpu.VMEM(gates.shape, gates.dtype),
            pltpu.VMEM(tokens.shape, tokens.dtype),
            pltpu.SemaphoreType.DMA((3 + 2 * (width // STEP),)),
        ],
        compiler_params=pltpu.CompilerParams(vmem_limit_bytes=16 * MIB),
        cost_estimate=expert_cost(36 * count, features, width),
        name="own_hidden",
    )(*[in_hbm(v) for v in (tokens, ids, gates, gate, up)])


def own_answer_kernel(experts, hidden_ref, terms_ref, down_hbm, out_ref, down_ref, done):
    features = down_ref.shape[1]
    copies = []
    for i, at in enumerate(range(0, features, 2 * STEP)):
        columns = pl.ds(at, 2 * STEP)
        copies.append(pltpu.make_async_copy(down_hbm.at[:, columns], down_ref.at[:, columns], done.at[i]))
    for copy in copies:
        copy.start()
    weight = row_weights(terms_ref[...], experts, 0)
    hidden = hidden_ref[...]
    for i, at in enumerate(range(0, features, 2 * STEP)):
        copies[i].wait()
        columns = slice(at, at + 2 * STEP)
        out_ref[:, columns] = jnp.dot(hidden, down_ref[:, columns], preferred_element_type=jnp.float32) * weight


def own_answer(hidden, terms, down, experts):
    count, width = hidden.shape
    features = down.shape[1]
    return pl.pallas_call(
        functools.partial(own_answer_kernel, experts),
        out_shape=[jax.ShapeDtypeStruct((count, features), jnp.float32), jax.ShapeDtypeStruct(down.shape, down.dtype)],
        in_specs=[whole()] * 2 + [anywhere()],
        out_specs=[whole()] * 2,
        scratch_shapes=[pltpu.SemaphoreType.DMA((features // (2 * STEP),))],
        compiler_params=pltpu.CompilerParams(vmem_limit_bytes=16 * MIB),
        cost_estimate=expert_cost(count, features, width // 3),
        name="own_answer",
    )(in_vmem(hidden), in_vmem(terms), in_hbm(down))


def nothing(*refs):
    pass


def held(*values, after=()):
    return pl.pallas_call(
        nothing,
        out_shape=[jax.ShapeDtypeStruct(v.shape, v.dtype) for v in values],
        in_specs=[anywhere()] * (len(values) + len(after)),
        out_specs=[anywhere()] * len(values),
        input_output_aliases={i: i for i in range(len(values))},
        compiler_params=pltpu.CompilerParams(vmem_limit_bytes=MIB),
        cost_estimate=pl.CostEstimate(flops=0, bytes_accessed=0, transcendentals=0),
        name="held",
    )(*values, *after)


def append_kernel(rows_ref, terms_ref, *refs):
    put_blocks(rows_ref[...], terms_ref[...], refs[-1])


def append(rows, terms, *after):
    count, features = rows.shape
    return pl.pallas_call(
        append_kernel,
        out_shape=jax.ShapeDtypeStruct((features + terms.shape[0], LANES), rows.dtype),
        in_specs=[whole()] * 2 + [anywhere()] * len(after),
        out_specs=whole(),
        compiler_params=pltpu.CompilerParams(vmem_limit_bytes=16 * MIB),
        cost_estimate=pl.CostEstimate(flops=0, bytes_accessed=4 * count * features, transcendentals=0),
        name="append",
    )(in_vmem(rows), in_vmem(terms), *after)


def expert_cost(count, features, width):
    return pl.CostEstimate(
        flops=6 * count * features * width, bytes_accessed=count * features * 4, transcendentals=count * width
    )


def expert_kernel(experts, other, added, after, parts, *refs):
    gate_ref, up_ref, down_ref, blocks_ref = refs[:4]
    added_refs = refs[4 : 4 + added * parts]
    out_refs = refs[4 + added * parts + after : -1]
    hidden_ref = refs[-1]
    features, width = gate_ref.shape
    rows = rows_of(blocks_ref, features)
    weight = row_weights(terms_of(blocks_ref, features), experts, other)
    for at in range(0, width, STEP):
        columns = slice(at, at + STEP)
        hidden_ref[:, columns] = hidden_columns(rows, gate_ref, up_ref, columns)
    hidden = hidden_ref[...]
    for at in range(0, features, 2 * STEP):
        columns = slice(at, at + 2 * STEP)
        answer = jnp.dot(hidden, down_ref[:, columns], preferred_element_type=jnp.float32) * weight
        start = 0
        for i, out_ref in enumerate(out_refs):
            part = answer[start : start + out_ref.shape[0]]
            for ref in added_refs[i::parts]:
                part = part + ref[:, columns].astype(jnp.float32)
            out_ref[:, columns] = part.astype(out_ref.dtype)
            start += out_ref.shape[0]


def run_expert(weights, other, experts, blocks, kind, *added, parts=1, after=()):
    features, width = weights[0].shape
    count = LANES
    operands = [in_vmem(v) for v in (*weights, blocks, *(v for group in added for v in group))]
    return pl.pallas_call(
        functools.partial(expert_kernel, experts, other, len(added), len(after), parts),
        out_shape=[jax.ShapeDtypeStruct((count // parts, features), kind)] * parts,
        in_specs=[whole()] * len(operands) + [anywhere()] * len(after),
        out_specs=[whole()] * parts,
        scratch_shapes=[pltpu.VMEM((count, width), jnp.bfloat16)],
        compiler_params=pltpu.CompilerParams(vmem_limit_bytes=16 * MIB),
        cost_estimate=expert_cost(count, features, width),
        name="expert",
    )(*operands, *after)


def sum_kernel(first_ref, second_ref, *refs):
    refs[-1][...] = (first_ref[...].astype(jnp.float32) + second_ref[...].astype(jnp.float32)).astype(refs[-1].dtype)


def sums(first, second, after=()):
    return pl.pallas_call(
        sum_kernel,
        out_shape=jax.ShapeDtypeStruct(first.shape, jnp.bfloat16),
        in_specs=[whole()] * 2 + [anywhere()] * len(after),
        out_specs=whole(),
        compiler_params=pltpu.CompilerParams(vmem_limit_bytes=16 * MIB),
        name="sums",
    )(in_vmem(first), in_vmem(second), *after)


def finish_kernel(pieces, total_ref, upper_ref, lower_ref, out_hbm, out, done):
    count = total_ref.shape[0] // pieces
    half = upper_ref.shape[0]
    copies = []
    for i in range(pieces):
        start = i * count
        ref, at = (upper_ref, start) if start < half else (lower_ref, start - half)
        part = total_ref[start : start + count] + ref[at : at + count].astype(jnp.float32)
        out[start : start + count] = part.astype(out.dtype)
        rows = pl.ds(start, count)
        copies.append(pltpu.make_async_copy(out.at[rows], out_hbm.at[rows], done.at[i]))
        copies[-1].start()
    for copy in copies:
        copy.wait()


def finish(total, upper, lower, pieces=4):
    return pl.pallas_call(
        functools.partial(finish_kernel, pieces),
        out_shape=jax.ShapeDtypeStruct(total.shape, upper.dtype),
        in_specs=[whole()] * 3,
        out_specs=anywhere(),
        scratch_shapes=[pltpu.VMEM(total.shape, upper.dtype), pltpu.SemaphoreType.DMA((pieces,))],
        compiler_params=pltpu.CompilerParams(vmem_limit_bytes=16 * MIB),
        cost_estimate=pl.CostEstimate(flops=0, bytes_accessed=4 * total.size, transcendentals=0),
        name="finish",
    )(in_vmem(total), in_vmem(upper), in_vmem(lower))


def on_four_chips(tokens, expert_ids, gate_values, w_gate, w_up, w_down):
    experts = lax.axis_size("expert")
    weights = (w_gate[0], w_up[0], w_down[0])
    wide, narrow = jnp.float32, jnp.bfloat16
    far = tuple(swap(w, (CORE, CORE)) for w in weights)
    first = swap(tokens, FIRST)
    own, terms, hidden, near_gate, near_up = own_hidden(tokens, expert_ids, gate_values, *weights[:2], experts)
    second = swap(own, SECOND)
    terms, = held(terms, after=far[:1])
    near_own, near_down = own_answer(hidden, terms, weights[2], experts)
    first = append(first, swap(terms, FIRST), near_own)
    third = swap(first, SECOND)

    near = (near_gate, near_up, near_down)
    near_run = functools.partial(run_expert, near, 0, experts)
    far_run = functools.partial(run_expert, far, CORE, experts)
    near_first = near_run(first, wide, parts=2, after=[near_own])
    near_second = near_run(second, wide, after=near_first)
    sum_second = far_run(second, narrow, near_second)
    back_second = swap(sum_second[0], SECOND)
    near_third = near_run(third, wide, parts=2, after=sum_second)
    sum_third = far_run(third, narrow, near_third, parts=2)
    passed_a, passed_b = swap(sum_third[0], SECOND), swap(sum_third[1], SECOND)
    sum_first = far_run(first, wide, near_first, parts=2, after=sum_third)
    sum_own = far_run(own, wide, [near_own], [back_second], after=sum_first)[0]
    back_first_a = swap(sums(sum_first[0], passed_a, after=[sum_own]), FIRST)
    back_first_b = swap(sums(sum_first[1], passed_b, after=[sum_own]), FIRST)
    return finish(sum_own, back_first_a, back_first_b)


def expert_apply(row_block, gate_matrix, up_matrix, down_matrix):
    gate_part = jnp.dot(row_block, gate_matrix, preferred_element_type=jnp.float32)
    up_part = jnp.dot(row_block, up_matrix, preferred_element_type=jnp.float32)
    hidden = (jax.nn.silu(gate_part) * up_part).astype(jnp.bfloat16)
    return jnp.dot(hidden, down_matrix, preferred_element_type=jnp.float32).astype(jnp.bfloat16)


def dispatched(tokens, expert_ids, gate_values, w_gate, w_up, w_down):
    token_count, features = tokens.shape
    topk_width = expert_ids.shape[1]
    experts_all = lax.axis_size("expert")
    pair_ids = expert_ids.reshape(-1)
    pair_rows = jnp.arange(pair_ids.shape[0], dtype=jnp.int32) // topk_width
    other_bound = min(
        token_count,
        ((topk_width - 1) * token_count + experts_all - 3) // (experts_all - 2) * 3 // 2,
    )
    slot_bound = max(token_count * 9 // 16, other_bound)
    one_hot = (pair_ids[:, None] == jnp.arange(experts_all, dtype=jnp.int32)[None, :]).astype(jnp.int32)
    earlier = jnp.cumsum(one_hot, axis=0) - one_hot
    places = pair_ids * slot_bound + jnp.sum(earlier * one_hot, axis=1)
    padded_source = jnp.concatenate([tokens, jnp.zeros((1, features), tokens.dtype)], axis=0)
    slot_table = (
        jnp.full((experts_all * slot_bound,), token_count, jnp.int32).at[places].set(pair_rows, mode="drop")
    )
    outgoing = padded_source[slot_table].reshape(experts_all, slot_bound, features)
    received = lax.all_to_all(outgoing, "expert", split_axis=0, concat_axis=0, tiled=True)
    answer = expert_apply(received.reshape(-1, features), w_gate[0], w_up[0], w_down[0])
    returned = lax.all_to_all(
        answer.reshape(received.shape), "expert", split_axis=0, concat_axis=0, tiled=True
    ).reshape(-1, features)[places]
    weighted = gate_values.reshape(-1)[:, None] * returned.astype(jnp.float32)
    return jnp.sum(weighted.reshape(token_count, topk_width, features), axis=1).astype(jnp.bfloat16)


def solution(mesh):
    placed = (
        P(("dp", "expert"), None),
        P(("dp", "expert"), None),
        P(("dp", "expert"), None),
        P("expert", None, None),
        P("expert", None, None),
        P("expert", None, None),
    )
    def body(tokens, *others):
        here = mesh.shape["expert"] == 8 and tokens.shape[0] == LANES
        return (on_four_chips if here else dispatched)(tokens, *others)

    return jax.shard_map(
        body, mesh=mesh, in_specs=placed, out_specs=P(("dp", "expert"), None), check_vma=False
    )
```

```python
import functools

import jax
import jax.numpy as jnp
from jax import lax
from jax.experimental import pallas as pl
from jax.experimental.pallas import tpu as pltpu
from jax.sharding import PartitionSpec as P

CORE, X, Y = 1, 2, 4
FIRST, SECOND = (X, Y), (Y, X)
LANES = 128
TERMS = 16
HERE, THERE = 0, 2
STEP = 256
MIB = 2**20


def in_vmem(value):
    return pltpu.with_memory_space_constraint(value, pltpu.VMEM)


def in_hbm(value):
    return pltpu.with_memory_space_constraint(value, pltpu.HBM)


def anywhere():
    return pl.BlockSpec(memory_space=pl.ANY)


def whole():
    return pl.BlockSpec(memory_space=pltpu.VMEM)


def swap(value, offsets):
    size = lax.axis_size("expert")
    return lax.ppermute(value, "expert", [(i, i ^ offsets[i % 2]) for i in range(size)])


def row_terms(ids, gates, pairs):
    topk, rows = ids.shape
    line = lax.broadcasted_iota(jnp.int32, (TERMS, rows), 0)
    slot = line
    for _ in range(3):
        slot = jnp.where(slot >= 4, slot - 4, slot)
    apart = jnp.where(slot >= 2, pairs[1], pairs[0]) ^ jnp.where((slot == 1) | (slot == 3), CORE, 0)
    expert = apart ^ lax.axis_index("expert")
    weight = jnp.zeros(line.shape, jnp.float32)
    for k in range(topk):
        weight += jnp.where(expert == ids[k : k + 1, :], gates[k : k + 1, :], 0.0)
    high = weight.astype(jnp.bfloat16).astype(jnp.float32)
    rest = weight - high
    middle = rest.astype(jnp.bfloat16).astype(jnp.float32)
    low = rest - middle
    terms = jnp.where(line < 4, high, jnp.where(line < 8, middle, low))
    return jnp.where(line < 12, terms, 0.0).astype(jnp.bfloat16)


def row_weights(terms, slot):
    count = terms.shape[1]
    line = lax.broadcasted_iota(jnp.int32, terms.shape, 0)
    chosen = (line == slot) | (line == slot + 4) | (line == slot + 8)
    weights = jnp.sum(jnp.where(chosen, terms.astype(jnp.float32), 0.0), axis=0, keepdims=True)
    square = (count, count)
    same = lax.broadcasted_iota(jnp.int32, square, 0) == lax.broadcasted_iota(jnp.int32, square, 1)
    return jnp.sum(jnp.where(same, jnp.broadcast_to(weights, square), 0.0), axis=1, keepdims=True)


def put_blocks(rows, terms, out_ref):
    count, features = rows.shape
    for i in range(features // LANES):
        out_ref[i * count : (i + 1) * count, :] = rows[:, i * LANES : (i + 1) * LANES]
    out_ref[features // LANES * count :, :] = terms


def rows_of(blocks_ref, features):
    count = LANES
    return jnp.concatenate([blocks_ref[i * count : (i + 1) * count, :] for i in range(features // LANES)], axis=1)


def terms_of(blocks_ref, features):
    return blocks_ref[features:, :]


def hidden_columns(rows, gate_ref, up_ref, columns):
    gate = jnp.dot(rows, gate_ref[:, columns], preferred_element_type=jnp.float32)
    up = jnp.dot(rows, up_ref[:, columns], preferred_element_type=jnp.float32)
    return (gate / (1.0 + jnp.exp(-gate)) * up).astype(jnp.bfloat16)


def own_hidden_kernel(
    tokens_hbm, ids_hbm, gates_hbm, gate_hbm, up_hbm, blocks_ref, terms_ref, hidden_ref, gate_ref, up_ref, ids, gates, tokens, done
):
    width = gate_ref.shape[1]
    pairs = [(ids_hbm, ids), (gates_hbm, gates), (tokens_hbm, tokens)]
    for at in range(0, width, STEP):
        columns = pl.ds(at, STEP)
        pairs.append((gate_hbm.at[:, columns], gate_ref.at[:, columns]))
        pairs.append((up_hbm.at[:, columns], up_ref.at[:, columns]))
    copies = [pltpu.make_async_copy(a, b, done.at[i]) for i, (a, b) in enumerate(pairs)]
    for copy in copies:
        copy.start()
    copies[0].wait()
    copies[1].wait()
    on_first = lax.axis_index("expert") % 2 == 0
    first, second = jnp.where(on_first, X, Y), jnp.where(on_first, Y, X)
    terms_ref[...] = row_terms(ids, gates, (first, X ^ Y))
    terms = row_terms(ids, gates, (0, second))
    copies[2].wait()
    rows = tokens[...]
    put_blocks(rows, terms, blocks_ref)
    waits = iter(copies[3:])
    for at in range(0, width, STEP):
        next(waits).wait()
        next(waits).wait()
        columns = slice(at, at + STEP)
        hidden_ref[:, columns] = hidden_columns(rows, gate_ref, up_ref, columns)


def own_hidden(tokens, ids, gates, gate, up):
    count, features = tokens.shape
    width = gate.shape[1]
    ids, gates = ids.T, gates.T
    return pl.pallas_call(
        own_hidden_kernel,
        out_shape=[
            jax.ShapeDtypeStruct((features + TERMS, LANES), tokens.dtype),
            jax.ShapeDtypeStruct((TERMS, LANES), tokens.dtype),
            jax.ShapeDtypeStruct((count, width), tokens.dtype),
            jax.ShapeDtypeStruct(gate.shape, gate.dtype),
            jax.ShapeDtypeStruct(up.shape, up.dtype),
        ],
        in_specs=[anywhere()] * 5,
        out_specs=[whole()] * 5,
        scratch_shapes=[
            pltpu.VMEM(ids.shape, ids.dtype),
            pltpu.VMEM(gates.shape, gates.dtype),
            pltpu.VMEM(tokens.shape, tokens.dtype),
            pltpu.SemaphoreType.DMA((3 + 2 * (width // STEP),)),
        ],
        compiler_params=pltpu.CompilerParams(vmem_limit_bytes=16 * MIB),
        cost_estimate=expert_cost(36 * count, features, width),
        name="own_hidden",
    )(*[in_hbm(v) for v in (tokens, ids, gates, gate, up)])


def own_answer_kernel(hidden_ref, blocks_ref, down_hbm, out_ref, down_ref, done):
    features = down_ref.shape[1]
    copies = []
    for i, at in enumerate(range(0, features, 2 * STEP)):
        columns = pl.ds(at, 2 * STEP)
        copies.append(pltpu.make_async_copy(down_hbm.at[:, columns], down_ref.at[:, columns], done.at[i]))
    for copy in copies:
        copy.start()
    weight = row_weights(terms_of(blocks_ref, features), HERE)
    hidden = hidden_ref[...]
    for i, at in enumerate(range(0, features, 2 * STEP)):
        copies[i].wait()
        columns = slice(at, at + 2 * STEP)
        out_ref[:, columns] = jnp.dot(hidden, down_ref[:, columns], preferred_element_type=jnp.float32) * weight


def own_answer(hidden, blocks, down):
    count, width = hidden.shape
    features = down.shape[1]
    return pl.pallas_call(
        own_answer_kernel,
        out_shape=[jax.ShapeDtypeStruct((count, features), jnp.float32), jax.ShapeDtypeStruct(down.shape, down.dtype)],
        in_specs=[whole()] * 2 + [anywhere()],
        out_specs=[whole()] * 2,
        scratch_shapes=[pltpu.SemaphoreType.DMA((features // (2 * STEP),))],
        compiler_params=pltpu.CompilerParams(vmem_limit_bytes=16 * MIB),
        cost_estimate=expert_cost(count, features, width // 3),
        name="own_answer",
    )(in_vmem(hidden), in_vmem(blocks), in_hbm(down))


def nothing(*refs):
    pass


def held(*values, after=()):
    return pl.pallas_call(
        nothing,
        out_shape=[jax.ShapeDtypeStruct(v.shape, v.dtype) for v in values],
        in_specs=[anywhere()] * (len(values) + len(after)),
        out_specs=[anywhere()] * len(values),
        input_output_aliases={i: i for i in range(len(values))},
        compiler_params=pltpu.CompilerParams(vmem_limit_bytes=MIB),
        cost_estimate=pl.CostEstimate(flops=0, bytes_accessed=0, transcendentals=0),
        name="held",
    )(*values, *after)


def append_kernel(rows_ref, terms_ref, *refs):
    put_blocks(rows_ref[...], terms_ref[...], refs[-1])


def append(rows, terms, *after):
    count, features = rows.shape
    return pl.pallas_call(
        append_kernel,
        out_shape=jax.ShapeDtypeStruct((features + terms.shape[0], LANES), rows.dtype),
        in_specs=[whole()] * 2 + [anywhere()] * len(after),
        out_specs=whole(),
        compiler_params=pltpu.CompilerParams(vmem_limit_bytes=16 * MIB),
        cost_estimate=pl.CostEstimate(flops=0, bytes_accessed=4 * count * features, transcendentals=0),
        name="append",
    )(in_vmem(rows), in_vmem(terms), *after)


def expert_cost(count, features, width):
    return pl.CostEstimate(
        flops=6 * count * features * width, bytes_accessed=count * features * 4, transcendentals=count * width
    )


def expert_kernel(slot, added, after, parts, *refs):
    gate_ref, up_ref, down_ref, blocks_ref = refs[:4]
    added_refs = refs[4 : 4 + added * parts]
    out_refs = refs[4 + added * parts + after : -1]
    hidden_ref = refs[-1]
    features, width = gate_ref.shape
    rows = rows_of(blocks_ref, features)
    weight = row_weights(terms_of(blocks_ref, features), slot)
    for at in range(0, width, STEP):
        columns = slice(at, at + STEP)
        hidden_ref[:, columns] = hidden_columns(rows, gate_ref, up_ref, columns)
    hidden = hidden_ref[...]
    for at in range(0, features, 2 * STEP):
        columns = slice(at, at + 2 * STEP)
        answer = jnp.dot(hidden, down_ref[:, columns], preferred_element_type=jnp.float32) * weight
        start = 0
        for i, out_ref in enumerate(out_refs):
            part = answer[start : start + out_ref.shape[0]]
            for ref in added_refs[i::parts]:
                part = part + ref[:, columns].astype(jnp.float32)
            out_ref[:, columns] = part.astype(out_ref.dtype)
            start += out_ref.shape[0]


def run_expert(weights, slot, blocks, kind, *added, parts=1, after=()):
    features, width = weights[0].shape
    count = LANES
    operands = [in_vmem(v) for v in (*weights, blocks, *(v for group in added for v in group))]
    return pl.pallas_call(
        functools.partial(expert_kernel, slot, len(added), len(after), parts),
        out_shape=[jax.ShapeDtypeStruct((count // parts, features), kind)] * parts,
        in_specs=[whole()] * len(operands) + [anywhere()] * len(after),
        out_specs=[whole()] * parts,
        scratch_shapes=[pltpu.VMEM((count, width), jnp.bfloat16)],
        compiler_params=pltpu.CompilerParams(vmem_limit_bytes=16 * MIB),
        cost_estimate=expert_cost(count, features, width),
        name="expert",
    )(*operands, *after)


def sum_kernel(first_ref, second_ref, *refs):
    refs[-1][...] = (first_ref[...].astype(jnp.float32) + second_ref[...].astype(jnp.float32)).astype(refs[-1].dtype)


def sums(first, second, after=()):
    return pl.pallas_call(
        sum_kernel,
        out_shape=jax.ShapeDtypeStruct(first.shape, jnp.bfloat16),
        in_specs=[whole()] * 2 + [anywhere()] * len(after),
        out_specs=whole(),
        compiler_params=pltpu.CompilerParams(vmem_limit_bytes=16 * MIB),
        name="sums",
    )(in_vmem(first), in_vmem(second), *after)


def finish_kernel(pieces, total_ref, upper_ref, lower_ref, out_hbm, out, done):
    count = total_ref.shape[0] // pieces
    half = upper_ref.shape[0]
    copies = []
    for i in range(pieces):
        start = i * count
        ref, at = (upper_ref, start) if start < half else (lower_ref, start - half)
        part = total_ref[start : start + count] + ref[at : at + count].astype(jnp.float32)
        out[start : start + count] = part.astype(out.dtype)
        rows = pl.ds(start, count)
        copies.append(pltpu.make_async_copy(out.at[rows], out_hbm.at[rows], done.at[i]))
        copies[-1].start()
    for copy in copies:
        copy.wait()


def finish(total, upper, lower, pieces=4):
    return pl.pallas_call(
        functools.partial(finish_kernel, pieces),
        out_shape=jax.ShapeDtypeStruct(total.shape, upper.dtype),
        in_specs=[whole()] * 3,
        out_specs=anywhere(),
        scratch_shapes=[pltpu.VMEM(total.shape, upper.dtype), pltpu.SemaphoreType.DMA((pieces,))],
        compiler_params=pltpu.CompilerParams(vmem_limit_bytes=16 * MIB),
        cost_estimate=pl.CostEstimate(flops=0, bytes_accessed=4 * total.size, transcendentals=0),
        name="finish",
    )(in_vmem(total), in_vmem(upper), in_vmem(lower))


def on_four_chips(tokens, expert_ids, gate_values, w_gate, w_up, w_down):
    weights = (w_gate[0], w_up[0], w_down[0])
    wide, narrow = jnp.float32, jnp.bfloat16
    far = tuple(swap(w, (CORE, CORE)) for w in weights)
    first = swap(tokens, FIRST)
    own, terms, hidden, near_gate, near_up = own_hidden(tokens, expert_ids, gate_values, *weights[:2])
    second = swap(own, SECOND)
    terms, = held(terms, after=far[:1])
    near_own, near_down = own_answer(hidden, own, weights[2])
    first = append(first, swap(terms, FIRST), near_own)
    third = swap(first, SECOND)

    near = (near_gate, near_up, near_down)

    def near_run(chip, *given, **options):
        return run_expert(near, chip, *given, **options)

    def far_run(chip, *given, **options):
        return run_expert(far, chip + CORE, *given, **options)

    near_first = near_run(HERE, first, wide, parts=2, after=[near_own])
    near_second = near_run(THERE, second, wide, after=near_first)
    sum_second = far_run(THERE, second, narrow, near_second)
    back_second = swap(sum_second[0], SECOND)
    near_third = near_run(THERE, third, wide, parts=2, after=sum_second)
    sum_third = far_run(THERE, third, narrow, near_third, parts=2)
    passed_a, passed_b = swap(sum_third[0], SECOND), swap(sum_third[1], SECOND)
    sum_first = far_run(HERE, first, wide, near_first, parts=2, after=sum_third)
    sum_own = far_run(HERE, own, wide, [near_own], [back_second], after=sum_first)[0]
    back_first_a = swap(sums(sum_first[0], passed_a, after=[sum_own]), FIRST)
    back_first_b = swap(sums(sum_first[1], passed_b, after=[sum_own]), FIRST)
    return finish(sum_own, back_first_a, back_first_b)


def expert_apply(row_block, gate_matrix, up_matrix, down_matrix):
    gate_part = jnp.dot(row_block, gate_matrix, preferred_element_type=jnp.float32)
    up_part = jnp.dot(row_block, up_matrix, preferred_element_type=jnp.float32)
    hidden = (jax.nn.silu(gate_part) * up_part).astype(jnp.bfloat16)
    return jnp.dot(hidden, down_matrix, preferred_element_type=jnp.float32).astype(jnp.bfloat16)


def dispatched(tokens, expert_ids, gate_values, w_gate, w_up, w_down):
    token_count, features = tokens.shape
    topk_width = expert_ids.shape[1]
    experts_all = lax.axis_size("expert")
    pair_ids = expert_ids.reshape(-1)
    pair_rows = jnp.arange(pair_ids.shape[0], dtype=jnp.int32) // topk_width
    other_bound = min(
        token_count,
        ((topk_width - 1) * token_count + experts_all - 3) // (experts_all - 2) * 3 // 2,
    )
    slot_bound = max(token_count * 9 // 16, other_bound)
    one_hot = (pair_ids[:, None] == jnp.arange(experts_all, dtype=jnp.int32)[None, :]).astype(jnp.int32)
    earlier = jnp.cumsum(one_hot, axis=0) - one_hot
    places = pair_ids * slot_bound + jnp.sum(earlier * one_hot, axis=1)
    padded_source = jnp.concatenate([tokens, jnp.zeros((1, features), tokens.dtype)], axis=0)
    slot_table = (
        jnp.full((experts_all * slot_bound,), token_count, jnp.int32).at[places].set(pair_rows, mode="drop")
    )
    outgoing = padded_source[slot_table].reshape(experts_all, slot_bound, features)
    received = lax.all_to_all(outgoing, "expert", split_axis=0, concat_axis=0, tiled=True)
    answer = expert_apply(received.reshape(-1, features), w_gate[0], w_up[0], w_down[0])
    returned = lax.all_to_all(
        answer.reshape(received.shape), "expert", split_axis=0, concat_axis=0, tiled=True
    ).reshape(-1, features)[places]
    weighted = gate_values.reshape(-1)[:, None] * returned.astype(jnp.float32)
    return jnp.sum(weighted.reshape(token_count, topk_width, features), axis=1).astype(jnp.bfloat16)


def solution(mesh):
    placed = (
        P(("dp", "expert"), None),
        P(("dp", "expert"), None),
        P(("dp", "expert"), None),
        P("expert", None, None),
        P("expert", None, None),
        P("expert", None, None),
    )
    def body(tokens, *others):
        here = mesh.shape["expert"] == 8 and tokens.shape[0] == LANES
        return (on_four_chips if here else dispatched)(tokens, *others)

    return jax.shard_map(
        body, mesh=mesh, in_specs=placed, out_specs=P(("dp", "expert"), None), check_vma=False
    )
```

```python
import functools

import jax
import jax.numpy as jnp
from jax import lax
from jax.experimental import pallas as pl
from jax.experimental.pallas import tpu as pltpu
from jax.sharding import PartitionSpec as P

CORE, X, Y = 1, 2, 4
FIRST, SECOND = (X, Y), (Y, X)
LANES = 128
STEP = 256
MIB = 2**20


def in_vmem(value):
    return pltpu.with_memory_space_constraint(value, pltpu.VMEM)


def in_hbm(value):
    return pltpu.with_memory_space_constraint(value, pltpu.HBM)


def anywhere():
    return pl.BlockSpec(memory_space=pl.ANY)


def whole():
    return pl.BlockSpec(memory_space=pltpu.VMEM)


def swap(value, offsets):
    size = lax.axis_size("expert")
    return lax.ppermute(value, "expert", [(i, i ^ offsets[i % 2]) for i in range(size)])


def row_terms(ids, gates, experts):
    topk, rows = ids.shape
    line = lax.broadcasted_iota(jnp.int32, (4 * experts, rows), 0)
    expert = line
    for _ in range(3):
        expert = jnp.where(expert >= experts, expert - experts, expert)
    weight = jnp.zeros(line.shape, jnp.float32)
    for k in range(topk):
        weight += jnp.where(expert == ids[k : k + 1, :], gates[k : k + 1, :], 0.0)
    high = weight.astype(jnp.bfloat16).astype(jnp.float32)
    rest = weight - high
    middle = rest.astype(jnp.bfloat16).astype(jnp.float32)
    low = rest - middle
    terms = jnp.where(line < experts, high, jnp.where(line < 2 * experts, middle, low))
    return jnp.where(line < 3 * experts, terms, 0.0).astype(jnp.bfloat16)


def row_weights(terms, experts, other):
    count = terms.shape[1]
    line = lax.broadcasted_iota(jnp.int32, terms.shape, 0)
    own = lax.axis_index("expert") ^ other
    chosen = (line == own) | (line == own + experts) | (line == own + 2 * experts)
    weights = jnp.sum(jnp.where(chosen, terms.astype(jnp.float32), 0.0), axis=0, keepdims=True)
    square = (count, count)
    same = lax.broadcasted_iota(jnp.int32, square, 0) == lax.broadcasted_iota(jnp.int32, square, 1)
    return jnp.sum(jnp.where(same, jnp.broadcast_to(weights, square), 0.0), axis=1, keepdims=True)


def put_blocks(rows, terms, out_ref):
    count, features = rows.shape
    for i in range(features // LANES):
        out_ref[i * count : (i + 1) * count, :] = rows[:, i * LANES : (i + 1) * LANES]
    out_ref[features // LANES * count :, :] = terms


def rows_of(blocks_ref, features):
    count = LANES
    return jnp.concatenate([blocks_ref[i * count : (i + 1) * count, :] for i in range(features // LANES)], axis=1)


def terms_of(blocks_ref, features):
    return blocks_ref[features:, :]


def hidden_columns(rows, gate_ref, up_ref, columns):
    gate = jnp.dot(rows, gate_ref[:, columns], preferred_element_type=jnp.float32)
    up = jnp.dot(rows, up_ref[:, columns], preferred_element_type=jnp.float32)
    return (gate / (1.0 + jnp.exp(-gate)) * up).astype(jnp.bfloat16)


def own_hidden_kernel(
    experts, tokens_hbm, ids_hbm, gates_hbm, gate_hbm, up_hbm, blocks_ref, terms_ref, hidden_ref, gate_ref, up_ref, ids, gates, tokens, done
):
    width = gate_ref.shape[1]
    pairs = [(ids_hbm, ids), (gates_hbm, gates), (tokens_hbm, tokens)]
    for at in range(0, width, STEP):
        columns = pl.ds(at, STEP)
        pairs.append((gate_hbm.at[:, columns], gate_ref.at[:, columns]))
        pairs.append((up_hbm.at[:, columns], up_ref.at[:, columns]))
    copies = [pltpu.make_async_copy(a, b, done.at[i]) for i, (a, b) in enumerate(pairs)]
    for copy in copies:
        copy.start()
    copies[0].wait()
    copies[1].wait()
    terms = row_terms(ids, gates, experts)
    terms_ref[...] = terms
    copies[2].wait()
    rows = tokens[...]
    put_blocks(rows, terms, blocks_ref)
    waits = iter(copies[3:])
    for at in range(0, width, STEP):
        next(waits).wait()
        next(waits).wait()
        columns = slice(at, at + STEP)
        hidden_ref[:, columns] = hidden_columns(rows, gate_ref, up_ref, columns)


def own_hidden(tokens, ids, gates, gate, up, experts):
    count, features = tokens.shape
    width = gate.shape[1]
    ids, gates = ids.T, gates.T
    return pl.pallas_call(
        functools.partial(own_hidden_kernel, experts),
        out_shape=[
            jax.ShapeDtypeStruct((features + 4 * experts, LANES), tokens.dtype),
            jax.ShapeDtypeStruct((4 * experts, LANES), tokens.dtype),
            jax.ShapeDtypeStruct((count, width), tokens.dtype),
            jax.ShapeDtypeStruct(gate.shape, gate.dtype),
            jax.ShapeDtypeStruct(up.shape, up.dtype),
        ],
        in_specs=[anywhere()] * 5,
        out_specs=[whole()] * 5,
        scratch_shapes=[
            pltpu.VMEM(ids.shape, ids.dtype),
            pltpu.VMEM(gates.shape, gates.dtype),
            pltpu.VMEM(tokens.shape, tokens.dtype),
            pltpu.SemaphoreType.DMA((3 + 2 * (width // STEP),)),
        ],
        compiler_params=pltpu.CompilerParams(vmem_limit_bytes=16 * MIB),
        cost_estimate=expert_cost(36 * count, features, width),
        name="own_hidden",
    )(*[in_hbm(v) for v in (tokens, ids, gates, gate, up)])


def own_answer_kernel(experts, hidden_ref, terms_ref, down_hbm, out_ref, down_ref, done):
    features = down_ref.shape[1]
    copies = []
    for i, at in enumerate(range(0, features, 2 * STEP)):
        columns = pl.ds(at, 2 * STEP)
        copies.append(pltpu.make_async_copy(down_hbm.at[:, columns], down_ref.at[:, columns], done.at[i]))
    for copy in copies:
        copy.start()
    weight = row_weights(terms_ref[...], experts, 0)
    hidden = hidden_ref[...]
    for i, at in enumerate(range(0, features, 2 * STEP)):
        copies[i].wait()
        columns = slice(at, at + 2 * STEP)
        out_ref[:, columns] = jnp.dot(hidden, down_ref[:, columns], preferred_element_type=jnp.float32) * weight


def own_answer(hidden, terms, down, experts):
    count, width = hidden.shape
    features = down.shape[1]
    return pl.pallas_call(
        functools.partial(own_answer_kernel, experts),
        out_shape=[jax.ShapeDtypeStruct((count, features), jnp.float32), jax.ShapeDtypeStruct(down.shape, down.dtype)],
        in_specs=[whole()] * 2 + [anywhere()],
        out_specs=[whole()] * 2,
        scratch_shapes=[pltpu.SemaphoreType.DMA((features // (2 * STEP),))],
        compiler_params=pltpu.CompilerParams(vmem_limit_bytes=16 * MIB),
        cost_estimate=expert_cost(count, features, width // 3),
        name="own_answer",
    )(in_vmem(hidden), in_vmem(terms), in_hbm(down))


def nothing(*refs):
    pass


def held(*values, after=()):
    return pl.pallas_call(
        nothing,
        out_shape=[jax.ShapeDtypeStruct(v.shape, v.dtype) for v in values],
        in_specs=[anywhere()] * (len(values) + len(after)),
        out_specs=[anywhere()] * len(values),
        input_output_aliases={i: i for i in range(len(values))},
        compiler_params=pltpu.CompilerParams(vmem_limit_bytes=MIB),
        cost_estimate=pl.CostEstimate(flops=0, bytes_accessed=0, transcendentals=0),
        name="held",
    )(*values, *after)


def append_kernel(rows_ref, terms_ref, *refs):
    put_blocks(rows_ref[...], terms_ref[...], refs[-1])


def append(rows, terms, *after):
    count, features = rows.shape
    return pl.pallas_call(
        append_kernel,
        out_shape=jax.ShapeDtypeStruct((features + terms.shape[0], LANES), rows.dtype),
        in_specs=[whole()] * 2 + [anywhere()] * len(after),
        out_specs=whole(),
        compiler_params=pltpu.CompilerParams(vmem_limit_bytes=16 * MIB),
        cost_estimate=pl.CostEstimate(flops=0, bytes_accessed=4 * count * features, transcendentals=0),
        name="append",
    )(in_vmem(rows), in_vmem(terms), *after)


def expert_cost(count, features, width):
    return pl.CostEstimate(
        flops=6 * count * features * width, bytes_accessed=count * features * 4, transcendentals=count * width
    )


def expert_kernel(experts, other, added, after, parts, *refs):
    gate_ref, up_ref, down_ref, blocks_ref = refs[:4]
    added_refs = refs[4 : 4 + added * parts]
    out_refs = refs[4 + added * parts + after : -1]
    hidden_ref = refs[-1]
    features, width = gate_ref.shape
    rows = rows_of(blocks_ref, features)
    weight = row_weights(terms_of(blocks_ref, features), experts, other)
    for at in range(0, width, STEP):
        columns = slice(at, at + STEP)
        hidden_ref[:, columns] = hidden_columns(rows, gate_ref, up_ref, columns)
    hidden = hidden_ref[...]
    for at in range(0, features, 2 * STEP):
        columns = slice(at, at + 2 * STEP)
        answer = jnp.dot(hidden, down_ref[:, columns], preferred_element_type=jnp.float32) * weight
        start = 0
        for i, out_ref in enumerate(out_refs):
            part = answer[start : start + out_ref.shape[0]]
            for ref in added_refs[i::parts]:
                part = part + ref[:, columns].astype(jnp.float32)
            out_ref[:, columns] = part.astype(out_ref.dtype)
            start += out_ref.shape[0]


def run_expert(weights, other, experts, blocks, kind, *added, parts=1, after=()):
    features, width = weights[0].shape
    count = LANES
    operands = [in_vmem(v) for v in (*weights, blocks, *(v for group in added for v in group))]
    return pl.pallas_call(
        functools.partial(expert_kernel, experts, other, len(added), len(after), parts),
        out_shape=[jax.ShapeDtypeStruct((count // parts, features), kind)] * parts,
        in_specs=[whole()] * len(operands) + [anywhere()] * len(after),
        out_specs=[whole()] * parts,
        scratch_shapes=[pltpu.VMEM((count, width), jnp.bfloat16)],
        compiler_params=pltpu.CompilerParams(vmem_limit_bytes=16 * MIB),
        cost_estimate=expert_cost(count, features, width),
        name="expert",
    )(*operands, *after)


def sum_kernel(first_ref, second_ref, *refs):
    refs[-1][...] = (first_ref[...].astype(jnp.float32) + second_ref[...].astype(jnp.float32)).astype(refs[-1].dtype)


def sums(first, second, after=()):
    return pl.pallas_call(
        sum_kernel,
        out_shape=jax.ShapeDtypeStruct(first.shape, jnp.bfloat16),
        in_specs=[whole()] * 2 + [anywhere()] * len(after),
        out_specs=whole(),
        compiler_params=pltpu.CompilerParams(vmem_limit_bytes=16 * MIB),
        name="sums",
    )(in_vmem(first), in_vmem(second), *after)


def finish_kernel(pieces, total_ref, upper_ref, lower_ref, out_hbm, out, done):
    count = total_ref.shape[0] // pieces
    half = upper_ref.shape[0]
    copies = []
    for i in range(pieces):
        start = i * count
        ref, at = (upper_ref, start) if start < half else (lower_ref, start - half)
        part = total_ref[start : start + count] + ref[at : at + count].astype(jnp.float32)
        out[start : start + count] = part.astype(out.dtype)
        rows = pl.ds(start, count)
        copies.append(pltpu.make_async_copy(out.at[rows], out_hbm.at[rows], done.at[i]))
        copies[-1].start()
    for copy in copies:
        copy.wait()


def finish(total, upper, lower, pieces=4):
    return pl.pallas_call(
        functools.partial(finish_kernel, pieces),
        out_shape=jax.ShapeDtypeStruct(total.shape, upper.dtype),
        in_specs=[whole()] * 3,
        out_specs=anywhere(),
        scratch_shapes=[pltpu.VMEM(total.shape, upper.dtype), pltpu.SemaphoreType.DMA((pieces,))],
        compiler_params=pltpu.CompilerParams(vmem_limit_bytes=16 * MIB),
        cost_estimate=pl.CostEstimate(flops=0, bytes_accessed=4 * total.size, transcendentals=0),
        name="finish",
    )(in_vmem(total), in_vmem(upper), in_vmem(lower))


def on_four_chips(tokens, expert_ids, gate_values, w_gate, w_up, w_down):
    experts = lax.axis_size("expert")
    weights = (w_gate[0], w_up[0], w_down[0])
    wide, narrow = jnp.float32, jnp.bfloat16
    far = tuple(swap(w, (CORE, CORE)) for w in weights)
    first = swap(tokens, FIRST)
    own, terms, hidden, near_gate, near_up = own_hidden(tokens, expert_ids, gate_values, *weights[:2], experts)
    second = swap(own, SECOND)
    terms, = held(terms, after=far[:1])
    near_own, near_down = own_answer(hidden, terms, weights[2], experts)
    first = append(first, swap(terms, FIRST), near_own)
    third = swap(first, SECOND)

    near = (near_gate, near_up, near_down)
    near_run = functools.partial(run_expert, near, 0, experts)
    far_run = functools.partial(run_expert, far, CORE, experts)
    near_first = near_run(first, wide, parts=2, after=[near_own])
    near_second = near_run(second, wide, after=near_first)
    sum_second = far_run(second, narrow, near_second)
    back_second = swap(sum_second[0], SECOND)
    near_third = near_run(third, wide, parts=2, after=sum_second)
    sum_third = far_run(third, narrow, near_third, parts=2)
    passed_a, passed_b = swap(sum_third[0], SECOND), swap(sum_third[1], SECOND)
    sum_first = far_run(first, wide, near_first, parts=2, after=sum_third)
    sum_own = far_run(own, wide, [near_own], [back_second], after=sum_first)[0]
    back_first_a = swap(sums(sum_first[0], passed_a), FIRST)
    back_first_b = swap(sums(sum_first[1], passed_b), FIRST)
    return finish(sum_own, back_first_a, back_first_b)


def expert_apply(row_block, gate_matrix, up_matrix, down_matrix):
    gate_part = jnp.dot(row_block, gate_matrix, preferred_element_type=jnp.float32)
    up_part = jnp.dot(row_block, up_matrix, preferred_element_type=jnp.float32)
    hidden = (jax.nn.silu(gate_part) * up_part).astype(jnp.bfloat16)
    return jnp.dot(hidden, down_matrix, preferred_element_type=jnp.float32).astype(jnp.bfloat16)


def dispatched(tokens, expert_ids, gate_values, w_gate, w_up, w_down):
    token_count, features = tokens.shape
    topk_width = expert_ids.shape[1]
    experts_all = lax.axis_size("expert")
    pair_ids = expert_ids.reshape(-1)
    pair_rows = jnp.arange(pair_ids.shape[0], dtype=jnp.int32) // topk_width
    other_bound = min(
        token_count,
        ((topk_width - 1) * token_count + experts_all - 3) // (experts_all - 2) * 3 // 2,
    )
    slot_bound = max(token_count * 9 // 16, other_bound)
    one_hot = (pair_ids[:, None] == jnp.arange(experts_all, dtype=jnp.int32)[None, :]).astype(jnp.int32)
    earlier = jnp.cumsum(one_hot, axis=0) - one_hot
    places = pair_ids * slot_bound + jnp.sum(earlier * one_hot, axis=1)
    padded_source = jnp.concatenate([tokens, jnp.zeros((1, features), tokens.dtype)], axis=0)
    slot_table = (
        jnp.full((experts_all * slot_bound,), token_count, jnp.int32).at[places].set(pair_rows, mode="drop")
    )
    outgoing = padded_source[slot_table].reshape(experts_all, slot_bound, features)
    received = lax.all_to_all(outgoing, "expert", split_axis=0, concat_axis=0, tiled=True)
    answer = expert_apply(received.reshape(-1, features), w_gate[0], w_up[0], w_down[0])
    returned = lax.all_to_all(
        answer.reshape(received.shape), "expert", split_axis=0, concat_axis=0, tiled=True
    ).reshape(-1, features)[places]
    weighted = gate_values.reshape(-1)[:, None] * returned.astype(jnp.float32)
    return jnp.sum(weighted.reshape(token_count, topk_width, features), axis=1).astype(jnp.bfloat16)


def solution(mesh):
    placed = (
        P(("dp", "expert"), None),
        P(("dp", "expert"), None),
        P(("dp", "expert"), None),
        P("expert", None, None),
        P("expert", None, None),
        P("expert", None, None),
    )
    def body(tokens, *others):
        here = mesh.shape["expert"] == 8 and tokens.shape[0] == LANES
        return (on_four_chips if here else dispatched)(tokens, *others)

    return jax.shard_map(
        body, mesh=mesh, in_specs=placed, out_specs=P(("dp", "expert"), None), check_vma=False
    )
```

```python
import functools

import jax
import jax.numpy as jnp
from jax import lax
from jax.experimental import pallas as pl
from jax.experimental.pallas import tpu as pltpu
from jax.sharding import PartitionSpec as P

CORE, X, Y = 1, 2, 4
FIRST, SECOND = (Y, X), (X, Y)
LANES = 128
STEP = 256
MIB = 2**20


def in_vmem(value):
    return pltpu.with_memory_space_constraint(value, pltpu.VMEM)


def in_hbm(value):
    return pltpu.with_memory_space_constraint(value, pltpu.HBM)


def anywhere():
    return pl.BlockSpec(memory_space=pl.ANY)


def whole():
    return pl.BlockSpec(memory_space=pltpu.VMEM)


def swap(value, offsets):
    size = lax.axis_size("expert")
    return lax.ppermute(value, "expert", [(i, i ^ offsets[i % 2]) for i in range(size)])


def row_terms(ids, gates, experts):
    topk, rows = ids.shape
    line = lax.broadcasted_iota(jnp.int32, (4 * experts, rows), 0)
    expert = line
    for _ in range(3):
        expert = jnp.where(expert >= experts, expert - experts, expert)
    weight = jnp.zeros(line.shape, jnp.float32)
    for k in range(topk):
        weight += jnp.where(expert == ids[k : k + 1, :], gates[k : k + 1, :], 0.0)
    high = weight.astype(jnp.bfloat16).astype(jnp.float32)
    rest = weight - high
    middle = rest.astype(jnp.bfloat16).astype(jnp.float32)
    low = rest - middle
    terms = jnp.where(line < experts, high, jnp.where(line < 2 * experts, middle, low))
    return jnp.where(line < 3 * experts, terms, 0.0).astype(jnp.bfloat16)


def row_weights(terms, experts, other):
    count = terms.shape[1]
    line = lax.broadcasted_iota(jnp.int32, terms.shape, 0)
    own = lax.axis_index("expert") ^ other
    chosen = (line == own) | (line == own + experts) | (line == own + 2 * experts)
    weights = jnp.sum(jnp.where(chosen, terms.astype(jnp.float32), 0.0), axis=0, keepdims=True)
    square = (count, count)
    same = lax.broadcasted_iota(jnp.int32, square, 0) == lax.broadcasted_iota(jnp.int32, square, 1)
    return jnp.sum(jnp.where(same, jnp.broadcast_to(weights, square), 0.0), axis=1, keepdims=True)


def put_blocks(rows, terms, out_ref):
    count, features = rows.shape
    for i in range(features // LANES):
        out_ref[i * count : (i + 1) * count, :] = rows[:, i * LANES : (i + 1) * LANES]
    out_ref[features // LANES * count :, :] = terms


def rows_of(blocks_ref, features):
    count = LANES
    return jnp.concatenate([blocks_ref[i * count : (i + 1) * count, :] for i in range(features // LANES)], axis=1)


def terms_of(blocks_ref, features):
    return blocks_ref[features:, :]


def hidden_columns(rows, gate_ref, up_ref, columns):
    gate = jnp.dot(rows, gate_ref[:, columns], preferred_element_type=jnp.float32)
    up = jnp.dot(rows, up_ref[:, columns], preferred_element_type=jnp.float32)
    return (gate / (1.0 + jnp.exp(-gate)) * up).astype(jnp.bfloat16)


def own_hidden_kernel(
    experts, tokens_hbm, ids_hbm, gates_hbm, gate_hbm, up_hbm, blocks_ref, terms_ref, hidden_ref, gate_ref, up_ref, ids, gates, tokens, done
):
    width = gate_ref.shape[1]
    pairs = [(ids_hbm, ids), (gates_hbm, gates), (tokens_hbm, tokens)]
    for at in range(0, width, STEP):
        columns = pl.ds(at, STEP)
        pairs.append((gate_hbm.at[:, columns], gate_ref.at[:, columns]))
        pairs.append((up_hbm.at[:, columns], up_ref.at[:, columns]))
    copies = [pltpu.make_async_copy(a, b, done.at[i]) for i, (a, b) in enumerate(pairs)]
    for copy in copies:
        copy.start()
    copies[0].wait()
    copies[1].wait()
    terms = row_terms(ids, gates, experts)
    terms_ref[...] = terms
    copies[2].wait()
    rows = tokens[...]
    put_blocks(rows, terms, blocks_ref)
    waits = iter(copies[3:])
    for at in range(0, width, STEP):
        next(waits).wait()
        next(waits).wait()
        columns = slice(at, at + STEP)
        hidden_ref[:, columns] = hidden_columns(rows, gate_ref, up_ref, columns)


def own_hidden(tokens, ids, gates, gate, up, experts):
    count, features = tokens.shape
    width = gate.shape[1]
    ids, gates = ids.T, gates.T
    return pl.pallas_call(
        functools.partial(own_hidden_kernel, experts),
        out_shape=[
            jax.ShapeDtypeStruct((features + 4 * experts, LANES), tokens.dtype),
            jax.ShapeDtypeStruct((4 * experts, LANES), tokens.dtype),
            jax.ShapeDtypeStruct((count, width), tokens.dtype),
            jax.ShapeDtypeStruct(gate.shape, gate.dtype),
            jax.ShapeDtypeStruct(up.shape, up.dtype),
        ],
        in_specs=[anywhere()] * 5,
        out_specs=[whole()] * 5,
        scratch_shapes=[
            pltpu.VMEM(ids.shape, ids.dtype),
            pltpu.VMEM(gates.shape, gates.dtype),
            pltpu.VMEM(tokens.shape, tokens.dtype),
            pltpu.SemaphoreType.DMA((3 + 2 * (width // STEP),)),
        ],
        compiler_params=pltpu.CompilerParams(vmem_limit_bytes=16 * MIB),
        cost_estimate=expert_cost(36 * count, features, width),
        name="own_hidden",
    )(*[in_hbm(v) for v in (tokens, ids, gates, gate, up)])


def own_answer_kernel(experts, hidden_ref, terms_ref, down_hbm, out_ref, down_ref, done):
    features = down_ref.shape[1]
    copies = []
    for i, at in enumerate(range(0, features, 2 * STEP)):
        columns = pl.ds(at, 2 * STEP)
        copies.append(pltpu.make_async_copy(down_hbm.at[:, columns], down_ref.at[:, columns], done.at[i]))
    for copy in copies:
        copy.start()
    weight = row_weights(terms_ref[...], experts, 0)
    hidden = hidden_ref[...]
    for i, at in enumerate(range(0, features, 2 * STEP)):
        copies[i].wait()
        columns = slice(at, at + 2 * STEP)
        out_ref[:, columns] = jnp.dot(hidden, down_ref[:, columns], preferred_element_type=jnp.float32) * weight


def own_answer(hidden, terms, down, experts):
    count, width = hidden.shape
    features = down.shape[1]
    return pl.pallas_call(
        functools.partial(own_answer_kernel, experts),
        out_shape=[jax.ShapeDtypeStruct((count, features), jnp.float32), jax.ShapeDtypeStruct(down.shape, down.dtype)],
        in_specs=[whole()] * 2 + [anywhere()],
        out_specs=[whole()] * 2,
        scratch_shapes=[pltpu.SemaphoreType.DMA((features // (2 * STEP),))],
        compiler_params=pltpu.CompilerParams(vmem_limit_bytes=16 * MIB),
        cost_estimate=expert_cost(count, features, width // 3),
        name="own_answer",
    )(in_vmem(hidden), in_vmem(terms), in_hbm(down))


def nothing(*refs):
    pass


def held(*values, after=()):
    return pl.pallas_call(
        nothing,
        out_shape=[jax.ShapeDtypeStruct(v.shape, v.dtype) for v in values],
        in_specs=[anywhere()] * (len(values) + len(after)),
        out_specs=[anywhere()] * len(values),
        input_output_aliases={i: i for i in range(len(values))},
        compiler_params=pltpu.CompilerParams(vmem_limit_bytes=MIB),
        cost_estimate=pl.CostEstimate(flops=0, bytes_accessed=0, transcendentals=0),
        name="held",
    )(*values, *after)


def append_kernel(rows_ref, terms_ref, *refs):
    put_blocks(rows_ref[...], terms_ref[...], refs[-1])


def append(rows, terms, *after):
    count, features = rows.shape
    return pl.pallas_call(
        append_kernel,
        out_shape=jax.ShapeDtypeStruct((features + terms.shape[0], LANES), rows.dtype),
        in_specs=[whole()] * 2 + [anywhere()] * len(after),
        out_specs=whole(),
        compiler_params=pltpu.CompilerParams(vmem_limit_bytes=16 * MIB),
        cost_estimate=pl.CostEstimate(flops=0, bytes_accessed=4 * count * features, transcendentals=0),
        name="append",
    )(in_vmem(rows), in_vmem(terms), *after)


def expert_cost(count, features, width):
    return pl.CostEstimate(
        flops=6 * count * features * width, bytes_accessed=count * features * 4, transcendentals=count * width
    )


def expert_kernel(experts, other, added, after, parts, *refs):
    gate_ref, up_ref, down_ref, blocks_ref = refs[:4]
    added_refs = refs[4 : 4 + added * parts]
    out_refs = refs[4 + added * parts + after : -1]
    hidden_ref = refs[-1]
    features, width = gate_ref.shape
    rows = rows_of(blocks_ref, features)
    weight = row_weights(terms_of(blocks_ref, features), experts, other)
    for at in range(0, width, STEP):
        columns = slice(at, at + STEP)
        hidden_ref[:, columns] = hidden_columns(rows, gate_ref, up_ref, columns)
    hidden = hidden_ref[...]
    for at in range(0, features, 2 * STEP):
        columns = slice(at, at + 2 * STEP)
        answer = jnp.dot(hidden, down_ref[:, columns], preferred_element_type=jnp.float32) * weight
        start = 0
        for i, out_ref in enumerate(out_refs):
            part = answer[start : start + out_ref.shape[0]]
            for ref in added_refs[i::parts]:
                part = part + ref[:, columns].astype(jnp.float32)
            out_ref[:, columns] = part.astype(out_ref.dtype)
            start += out_ref.shape[0]


def run_expert(weights, other, experts, blocks, kind, *added, parts=1, after=()):
    features, width = weights[0].shape
    count = LANES
    operands = [in_vmem(v) for v in (*weights, blocks, *(v for group in added for v in group))]
    return pl.pallas_call(
        functools.partial(expert_kernel, experts, other, len(added), len(after), parts),
        out_shape=[jax.ShapeDtypeStruct((count // parts, features), kind)] * parts,
        in_specs=[whole()] * len(operands) + [anywhere()] * len(after),
        out_specs=[whole()] * parts,
        scratch_shapes=[pltpu.VMEM((count, width), jnp.bfloat16)],
        compiler_params=pltpu.CompilerParams(vmem_limit_bytes=16 * MIB),
        cost_estimate=expert_cost(count, features, width),
        name="expert",
    )(*operands, *after)


def sum_kernel(first_ref, second_ref, *refs):
    refs[-1][...] = (first_ref[...].astype(jnp.float32) + second_ref[...].astype(jnp.float32)).astype(refs[-1].dtype)


def sums(first, second, after=()):
    return pl.pallas_call(
        sum_kernel,
        out_shape=jax.ShapeDtypeStruct(first.shape, jnp.bfloat16),
        in_specs=[whole()] * 2 + [anywhere()] * len(after),
        out_specs=whole(),
        compiler_params=pltpu.CompilerParams(vmem_limit_bytes=16 * MIB),
        name="sums",
    )(in_vmem(first), in_vmem(second), *after)


def finish_kernel(pieces, total_ref, upper_ref, lower_ref, out_hbm, out, done):
    count = total_ref.shape[0] // pieces
    half = upper_ref.shape[0]
    copies = []
    for i in range(pieces):
        start = i * count
        ref, at = (upper_ref, start) if start < half else (lower_ref, start - half)
        part = total_ref[start : start + count] + ref[at : at + count].astype(jnp.float32)
        out[start : start + count] = part.astype(out.dtype)
        rows = pl.ds(start, count)
        copies.append(pltpu.make_async_copy(out.at[rows], out_hbm.at[rows], done.at[i]))
        copies[-1].start()
    for copy in copies:
        copy.wait()


def finish(total, upper, lower, pieces=4):
    return pl.pallas_call(
        functools.partial(finish_kernel, pieces),
        out_shape=jax.ShapeDtypeStruct(total.shape, upper.dtype),
        in_specs=[whole()] * 3,
        out_specs=anywhere(),
        scratch_shapes=[pltpu.VMEM(total.shape, upper.dtype), pltpu.SemaphoreType.DMA((pieces,))],
        compiler_params=pltpu.CompilerParams(vmem_limit_bytes=16 * MIB),
        cost_estimate=pl.CostEstimate(flops=0, bytes_accessed=4 * total.size, transcendentals=0),
        name="finish",
    )(in_vmem(total), in_vmem(upper), in_vmem(lower))


def on_four_chips(tokens, expert_ids, gate_values, w_gate, w_up, w_down):
    experts = lax.axis_size("expert")
    weights = (w_gate[0], w_up[0], w_down[0])
    wide, narrow = jnp.float32, jnp.bfloat16
    far = tuple(swap(w, (CORE, CORE)) for w in weights)
    first = swap(tokens, FIRST)
    own, terms, hidden, near_gate, near_up = own_hidden(tokens, expert_ids, gate_values, *weights[:2], experts)
    second = swap(own, SECOND)
    terms, = held(terms, after=far[:1])
    near_own, near_down = own_answer(hidden, terms, weights[2], experts)
    first = append(first, swap(terms, FIRST), near_own)
    third = swap(first, SECOND)

    near = (near_gate, near_up, near_down)
    near_run = functools.partial(run_expert, near, 0, experts)
    far_run = functools.partial(run_expert, far, CORE, experts)
    near_first = near_run(first, wide, parts=2, after=[near_own])
    near_second = near_run(second, wide, after=near_first)
    sum_second = far_run(second, narrow, near_second)
    back_second = swap(sum_second[0], SECOND)
    near_third = near_run(third, wide, parts=2, after=sum_second)
    sum_third = far_run(third, narrow, near_third, parts=2)
    passed_a, passed_b = swap(sum_third[0], SECOND), swap(sum_third[1], SECOND)
    sum_first = far_run(first, wide, near_first, parts=2, after=sum_third)
    sum_own = far_run(own, wide, [near_own], [back_second], after=sum_first)[0]
    back_first_a = swap(sums(sum_first[0], passed_a, after=[sum_own]), FIRST)
    back_first_b = swap(sums(sum_first[1], passed_b, after=[sum_own]), FIRST)
    return finish(sum_own, back_first_a, back_first_b)


def expert_apply(row_block, gate_matrix, up_matrix, down_matrix):
    gate_part = jnp.dot(row_block, gate_matrix, preferred_element_type=jnp.float32)
    up_part = jnp.dot(row_block, up_matrix, preferred_element_type=jnp.float32)
    hidden = (jax.nn.silu(gate_part) * up_part).astype(jnp.bfloat16)
    return jnp.dot(hidden, down_matrix, preferred_element_type=jnp.float32).astype(jnp.bfloat16)


def dispatched(tokens, expert_ids, gate_values, w_gate, w_up, w_down):
    token_count, features = tokens.shape
    topk_width = expert_ids.shape[1]
    experts_all = lax.axis_size("expert")
    pair_ids = expert_ids.reshape(-1)
    pair_rows = jnp.arange(pair_ids.shape[0], dtype=jnp.int32) // topk_width
    other_bound = min(
        token_count,
        ((topk_width - 1) * token_count + experts_all - 3) // (experts_all - 2) * 3 // 2,
    )
    slot_bound = max(token_count * 9 // 16, other_bound)
    one_hot = (pair_ids[:, None] == jnp.arange(experts_all, dtype=jnp.int32)[None, :]).astype(jnp.int32)
    earlier = jnp.cumsum(one_hot, axis=0) - one_hot
    places = pair_ids * slot_bound + jnp.sum(earlier * one_hot, axis=1)
    padded_source = jnp.concatenate([tokens, jnp.zeros((1, features), tokens.dtype)], axis=0)
    slot_table = (
        jnp.full((experts_all * slot_bound,), token_count, jnp.int32).at[places].set(pair_rows, mode="drop")
    )
    outgoing = padded_source[slot_table].reshape(experts_all, slot_bound, features)
    received = lax.all_to_all(outgoing, "expert", split_axis=0, concat_axis=0, tiled=True)
    answer = expert_apply(received.reshape(-1, features), w_gate[0], w_up[0], w_down[0])
    returned = lax.all_to_all(
        answer.reshape(received.shape), "expert", split_axis=0, concat_axis=0, tiled=True
    ).reshape(-1, features)[places]
    weighted = gate_values.reshape(-1)[:, None] * returned.astype(jnp.float32)
    return jnp.sum(weighted.reshape(token_count, topk_width, features), axis=1).astype(jnp.bfloat16)


def solution(mesh):
    placed = (
        P(("dp", "expert"), None),
        P(("dp", "expert"), None),
        P(("dp", "expert"), None),
        P("expert", None, None),
        P("expert", None, None),
        P("expert", None, None),
    )
    def body(tokens, *others):
        here = mesh.shape["expert"] == 8 and tokens.shape[0] == LANES
        return (on_four_chips if here else dispatched)(tokens, *others)

    return jax.shard_map(
        body, mesh=mesh, in_specs=placed, out_specs=P(("dp", "expert"), None), check_vma=False
    )
```

```python
import functools

import jax
import jax.numpy as jnp
from jax import lax
from jax.experimental import pallas as pl
from jax.experimental.pallas import tpu as pltpu
from jax.sharding import PartitionSpec as P

CORE, X, Y = 1, 2, 4
FIRST, SECOND = (Y, X), (X, Y)
LANES = 128
STEP = 256
MIB = 2**20


def in_vmem(value):
    return pltpu.with_memory_space_constraint(value, pltpu.VMEM)


def in_hbm(value):
    return pltpu.with_memory_space_constraint(value, pltpu.HBM)


def anywhere():
    return pl.BlockSpec(memory_space=pl.ANY)


def whole():
    return pl.BlockSpec(memory_space=pltpu.VMEM)


def swap(value, offsets):
    size = lax.axis_size("expert")
    return lax.ppermute(value, "expert", [(i, i ^ offsets[i % 2]) for i in range(size)])


def row_terms(ids, gates, experts):
    topk, rows = ids.shape
    line = lax.broadcasted_iota(jnp.int32, (4 * experts, rows), 0)
    expert = line
    for _ in range(3):
        expert = jnp.where(expert >= experts, expert - experts, expert)
    weight = jnp.zeros(line.shape, jnp.float32)
    for k in range(topk):
        weight += jnp.where(expert == ids[k : k + 1, :], gates[k : k + 1, :], 0.0)
    high = weight.astype(jnp.bfloat16).astype(jnp.float32)
    rest = weight - high
    middle = rest.astype(jnp.bfloat16).astype(jnp.float32)
    low = rest - middle
    terms = jnp.where(line < experts, high, jnp.where(line < 2 * experts, middle, low))
    return jnp.where(line < 3 * experts, terms, 0.0).astype(jnp.bfloat16)


def row_weights(terms, experts, other):
    count = terms.shape[1]
    line = lax.broadcasted_iota(jnp.int32, terms.shape, 0)
    own = lax.axis_index("expert") ^ other
    chosen = (line == own) | (line == own + experts) | (line == own + 2 * experts)
    weights = jnp.sum(jnp.where(chosen, terms.astype(jnp.float32), 0.0), axis=0, keepdims=True)
    square = (count, count)
    same = lax.broadcasted_iota(jnp.int32, square, 0) == lax.broadcasted_iota(jnp.int32, square, 1)
    return jnp.sum(jnp.where(same, jnp.broadcast_to(weights, square), 0.0), axis=1, keepdims=True)


def put_blocks(rows, terms, out_ref):
    count, features = rows.shape
    for i in range(features // LANES):
        out_ref[i * count : (i + 1) * count, :] = rows[:, i * LANES : (i + 1) * LANES]
    out_ref[features // LANES * count :, :] = terms


def rows_of(blocks_ref, features):
    count = LANES
    return jnp.concatenate([blocks_ref[i * count : (i + 1) * count, :] for i in range(features // LANES)], axis=1)


def terms_of(blocks_ref, features):
    return blocks_ref[features:, :]


def hidden_columns(rows, gate_ref, up_ref, columns):
    gate = jnp.dot(rows, gate_ref[:, columns], preferred_element_type=jnp.float32)
    up = jnp.dot(rows, up_ref[:, columns], preferred_element_type=jnp.float32)
    return (gate / (1.0 + jnp.exp(-gate)) * up).astype(jnp.bfloat16)


def own_hidden_kernel(
    experts, tokens_hbm, ids_hbm, gates_hbm, gate_hbm, up_hbm, blocks_ref, terms_ref, hidden_ref, gate_ref, up_ref, ids, gates, tokens, done
):
    width = gate_ref.shape[1]
    pairs = [(ids_hbm, ids), (gates_hbm, gates), (tokens_hbm, tokens)]
    for at in range(0, width, STEP):
        columns = pl.ds(at, STEP)
        pairs.append((gate_hbm.at[:, columns], gate_ref.at[:, columns]))
        pairs.append((up_hbm.at[:, columns], up_ref.at[:, columns]))
    copies = [pltpu.make_async_copy(a, b, done.at[i]) for i, (a, b) in enumerate(pairs)]
    for copy in copies:
        copy.start()
    copies[0].wait()
    copies[1].wait()
    terms = row_terms(ids, gates, experts)
    terms_ref[...] = terms
    copies[2].wait()
    rows = tokens[...]
    put_blocks(rows, terms, blocks_ref)
    waits = iter(copies[3:])
    for at in range(0, width, STEP):
        next(waits).wait()
        next(waits).wait()
        columns = slice(at, at + STEP)
        hidden_ref[:, columns] = hidden_columns(rows, gate_ref, up_ref, columns)


def own_hidden(tokens, ids, gates, gate, up, experts):
    count, features = tokens.shape
    width = gate.shape[1]
    ids, gates = ids.T, gates.T
    return pl.pallas_call(
        functools.partial(own_hidden_kernel, experts),
        out_shape=[
            jax.ShapeDtypeStruct((features + 4 * experts, LANES), tokens.dtype),
            jax.ShapeDtypeStruct((4 * experts, LANES), tokens.dtype),
            jax.ShapeDtypeStruct((count, width), tokens.dtype),
            jax.ShapeDtypeStruct(gate.shape, gate.dtype),
            jax.ShapeDtypeStruct(up.shape, up.dtype),
        ],
        in_specs=[anywhere()] * 5,
        out_specs=[whole()] * 5,
        scratch_shapes=[
            pltpu.VMEM(ids.shape, ids.dtype),
            pltpu.VMEM(gates.shape, gates.dtype),
            pltpu.VMEM(tokens.shape, tokens.dtype),
            pltpu.SemaphoreType.DMA((3 + 2 * (width // STEP),)),
        ],
        compiler_params=pltpu.CompilerParams(vmem_limit_bytes=16 * MIB),
        cost_estimate=expert_cost(36 * count, features, width),
        name="own_hidden",
    )(*[in_hbm(v) for v in (tokens, ids, gates, gate, up)])


def own_answer_kernel(experts, hidden_ref, terms_ref, down_hbm, out_ref, down_ref, done):
    features = down_ref.shape[1]
    copies = []
    for i, at in enumerate(range(0, features, 2 * STEP)):
        columns = pl.ds(at, 2 * STEP)
        copies.append(pltpu.make_async_copy(down_hbm.at[:, columns], down_ref.at[:, columns], done.at[i]))
    for copy in copies:
        copy.start()
    weight = row_weights(terms_ref[...], experts, 0)
    hidden = hidden_ref[...]
    for i, at in enumerate(range(0, features, 2 * STEP)):
        copies[i].wait()
        columns = slice(at, at + 2 * STEP)
        out_ref[:, columns] = jnp.dot(hidden, down_ref[:, columns], preferred_element_type=jnp.float32) * weight


def own_answer(hidden, terms, down, experts):
    count, width = hidden.shape
    features = down.shape[1]
    return pl.pallas_call(
        functools.partial(own_answer_kernel, experts),
        out_shape=[jax.ShapeDtypeStruct((count, features), jnp.float32), jax.ShapeDtypeStruct(down.shape, down.dtype)],
        in_specs=[whole()] * 2 + [anywhere()],
        out_specs=[whole()] * 2,
        scratch_shapes=[pltpu.SemaphoreType.DMA((features // (2 * STEP),))],
        compiler_params=pltpu.CompilerParams(vmem_limit_bytes=16 * MIB),
        cost_estimate=expert_cost(count, features, width // 3),
        name="own_answer",
    )(in_vmem(hidden), in_vmem(terms), in_hbm(down))


def nothing(*refs):
    pass


def held(*values, after=()):
    return pl.pallas_call(
        nothing,
        out_shape=[jax.ShapeDtypeStruct(v.shape, v.dtype) for v in values],
        in_specs=[anywhere()] * (len(values) + len(after)),
        out_specs=[anywhere()] * len(values),
        input_output_aliases={i: i for i in range(len(values))},
        compiler_params=pltpu.CompilerParams(vmem_limit_bytes=MIB),
        cost_estimate=pl.CostEstimate(flops=0, bytes_accessed=0, transcendentals=0),
        name="held",
    )(*values, *after)


def append_kernel(rows_ref, terms_ref, *refs):
    put_blocks(rows_ref[...], terms_ref[...], refs[-1])


def append(rows, terms, *after):
    count, features = rows.shape
    return pl.pallas_call(
        append_kernel,
        out_shape=jax.ShapeDtypeStruct((features + terms.shape[0], LANES), rows.dtype),
        in_specs=[whole()] * 2 + [anywhere()] * len(after),
        out_specs=whole(),
        compiler_params=pltpu.CompilerParams(vmem_limit_bytes=16 * MIB),
        cost_estimate=pl.CostEstimate(flops=0, bytes_accessed=4 * count * features, transcendentals=0),
        name="append",
    )(in_vmem(rows), in_vmem(terms), *after)


def expert_cost(count, features, width):
    return pl.CostEstimate(
        flops=6 * count * features * width, bytes_accessed=count * features * 4, transcendentals=count * width
    )


def expert_kernel(experts, other, added, after, parts, *refs):
    gate_ref, up_ref, down_ref, blocks_ref = refs[:4]
    added_refs = refs[4 : 4 + added * parts]
    out_refs = refs[4 + added * parts + after : -1]
    hidden_ref = refs[-1]
    features, width = gate_ref.shape
    rows = rows_of(blocks_ref, features)
    weight = row_weights(terms_of(blocks_ref, features), experts, other)
    for at in range(0, width, STEP):
        columns = slice(at, at + STEP)
        hidden_ref[:, columns] = hidden_columns(rows, gate_ref, up_ref, columns)
    hidden = hidden_ref[...]
    for at in range(0, features, 2 * STEP):
        columns = slice(at, at + 2 * STEP)
        answer = jnp.dot(hidden, down_ref[:, columns], preferred_element_type=jnp.float32) * weight
        start = 0
        for i, out_ref in enumerate(out_refs):
            part = answer[start : start + out_ref.shape[0]]
            for ref in added_refs[i::parts]:
                part = part + ref[:, columns].astype(jnp.float32)
            out_ref[:, columns] = part.astype(out_ref.dtype)
            start += out_ref.shape[0]


def run_expert(weights, other, experts, blocks, kind, *added, parts=1, after=()):
    features, width = weights[0].shape
    count = LANES
    operands = [in_vmem(v) for v in (*weights, blocks, *(v for group in added for v in group))]
    return pl.pallas_call(
        functools.partial(expert_kernel, experts, other, len(added), len(after), parts),
        out_shape=[jax.ShapeDtypeStruct((count // parts, features), kind)] * parts,
        in_specs=[whole()] * len(operands) + [anywhere()] * len(after),
        out_specs=[whole()] * parts,
        scratch_shapes=[pltpu.VMEM((count, width), jnp.bfloat16)],
        compiler_params=pltpu.CompilerParams(vmem_limit_bytes=16 * MIB),
        cost_estimate=expert_cost(count, features, width),
        name="expert",
    )(*operands, *after)


def sum_kernel(first_ref, second_ref, *refs):
    refs[-1][...] = (first_ref[...].astype(jnp.float32) + second_ref[...].astype(jnp.float32)).astype(refs[-1].dtype)


def sums(first, second, after=()):
    return pl.pallas_call(
        sum_kernel,
        out_shape=jax.ShapeDtypeStruct(first.shape, jnp.bfloat16),
        in_specs=[whole()] * 2 + [anywhere()] * len(after),
        out_specs=whole(),
        compiler_params=pltpu.CompilerParams(vmem_limit_bytes=16 * MIB),
        name="sums",
    )(in_vmem(first), in_vmem(second), *after)


def finish_kernel(pieces, total_ref, upper_ref, lower_ref, out_hbm, out, done):
    count = total_ref.shape[0] // pieces
    half = upper_ref.shape[0]
    copies = []
    for i in range(pieces):
        start = i * count
        ref, at = (upper_ref, start) if start < half else (lower_ref, start - half)
        part = total_ref[start : start + count] + ref[at : at + count].astype(jnp.float32)
        out[start : start + count] = part.astype(out.dtype)
        rows = pl.ds(start, count)
        copies.append(pltpu.make_async_copy(out.at[rows], out_hbm.at[rows], done.at[i]))
        copies[-1].start()
    for copy in copies:
        copy.wait()


def finish(total, upper, lower, pieces=4):
    return pl.pallas_call(
        functools.partial(finish_kernel, pieces),
        out_shape=jax.ShapeDtypeStruct(total.shape, upper.dtype),
        in_specs=[whole()] * 3,
        out_specs=anywhere(),
        scratch_shapes=[pltpu.VMEM(total.shape, upper.dtype), pltpu.SemaphoreType.DMA((pieces,))],
        compiler_params=pltpu.CompilerParams(vmem_limit_bytes=16 * MIB),
        cost_estimate=pl.CostEstimate(flops=0, bytes_accessed=4 * total.size, transcendentals=0),
        name="finish",
    )(in_vmem(total), in_vmem(upper), in_vmem(lower))


def on_four_chips(tokens, expert_ids, gate_values, w_gate, w_up, w_down):
    experts = lax.axis_size("expert")
    weights = (w_gate[0], w_up[0], w_down[0])
    wide, narrow = jnp.float32, jnp.bfloat16
    far = tuple(swap(w, (CORE, CORE)) for w in weights)
    first = swap(tokens, FIRST)
    own, terms, hidden, near_gate, near_up = own_hidden(tokens, expert_ids, gate_values, *weights[:2], experts)
    second = swap(own, SECOND)
    terms, = held(terms, after=far[:1])
    near_own, near_down = own_answer(hidden, terms, weights[2], experts)
    first = append(first, swap(terms, FIRST), near_own)
    third = swap(first, SECOND)

    near = (near_gate, near_up, near_down)
    near_run = functools.partial(run_expert, near, 0, experts)
    far_run = functools.partial(run_expert, far, CORE, experts)
    near_first = near_run(first, wide, parts=2, after=[near_own])
    near_second = near_run(second, wide, after=near_first)
    sum_second = far_run(second, narrow, near_second)
    back_second = swap(sum_second[0], SECOND)
    near_third = near_run(third, wide, parts=2, after=sum_second)
    sum_third = far_run(third, narrow, near_third, parts=2)
    passed_a, passed_b = swap(sum_third[0], SECOND), swap(sum_third[1], SECOND)
    sum_first = far_run(first, wide, near_first, parts=2, after=sum_third)
    sum_own = far_run(own, wide, [near_own], [back_second], after=sum_first)[0]
    back_first_a = swap(sums(sum_first[0], passed_a), FIRST)
    back_first_b = swap(sums(sum_first[1], passed_b), FIRST)
    return finish(sum_own, back_first_a, back_first_b)


def expert_apply(row_block, gate_matrix, up_matrix, down_matrix):
    gate_part = jnp.dot(row_block, gate_matrix, preferred_element_type=jnp.float32)
    up_part = jnp.dot(row_block, up_matrix, preferred_element_type=jnp.float32)
    hidden = (jax.nn.silu(gate_part) * up_part).astype(jnp.bfloat16)
    return jnp.dot(hidden, down_matrix, preferred_element_type=jnp.float32).astype(jnp.bfloat16)


def dispatched(tokens, expert_ids, gate_values, w_gate, w_up, w_down):
    token_count, features = tokens.shape
    topk_width = expert_ids.shape[1]
    experts_all = lax.axis_size("expert")
    pair_ids = expert_ids.reshape(-1)
    pair_rows = jnp.arange(pair_ids.shape[0], dtype=jnp.int32) // topk_width
    other_bound = min(
        token_count,
        ((topk_width - 1) * token_count + experts_all - 3) // (experts_all - 2) * 3 // 2,
    )
    slot_bound = max(token_count * 9 // 16, other_bound)
    one_hot = (pair_ids[:, None] == jnp.arange(experts_all, dtype=jnp.int32)[None, :]).astype(jnp.int32)
    earlier = jnp.cumsum(one_hot, axis=0) - one_hot
    places = pair_ids * slot_bound + jnp.sum(earlier * one_hot, axis=1)
    padded_source = jnp.concatenate([tokens, jnp.zeros((1, features), tokens.dtype)], axis=0)
    slot_table = (
        jnp.full((experts_all * slot_bound,), token_count, jnp.int32).at[places].set(pair_rows, mode="drop")
    )
    outgoing = padded_source[slot_table].reshape(experts_all, slot_bound, features)
    received = lax.all_to_all(outgoing, "expert", split_axis=0, concat_axis=0, tiled=True)
    answer = expert_apply(received.reshape(-1, features), w_gate[0], w_up[0], w_down[0])
    returned = lax.all_to_all(
        answer.reshape(received.shape), "expert", split_axis=0, concat_axis=0, tiled=True
    ).reshape(-1, features)[places]
    weighted = gate_values.reshape(-1)[:, None] * returned.astype(jnp.float32)
    return jnp.sum(weighted.reshape(token_count, topk_width, features), axis=1).astype(jnp.bfloat16)


def solution(mesh):
    placed = (
        P(("dp", "expert"), None),
        P(("dp", "expert"), None),
        P(("dp", "expert"), None),
        P("expert", None, None),
        P("expert", None, None),
        P("expert", None, None),
    )
    def body(tokens, *others):
        here = mesh.shape["expert"] == 8 and tokens.shape[0] == LANES
        return (on_four_chips if here else dispatched)(tokens, *others)

    return jax.shard_map(
        body, mesh=mesh, in_specs=placed, out_specs=P(("dp", "expert"), None), check_vma=False
    )
```
